512 devices in a mesh: row: 16 (over y_hi, x, core), col: 32 (over y_lo, z).
Axes of the slice: x: 4, y: 8 (y_hi: 2, y_lo: 4; y = y_hi * 4 + y_lo), z: 8, core: 2. Of those that a mesh axis runs over, the one named last changes fastest.
Arguments:
- tokens_fwd: bfloat16 [512, 12288], P('col', 'row'), may hold values from -6 to 6
- tokens_bwd: bfloat16 [512, 12288], P('col', 'row'), may hold values from -6 to 6
- weight: bfloat16 [12288, 24576], P('row', 'col'), may hold values from -0.0546875 to 0.0546875
- bias: float32 [24576], P('col'), may hold values from -3 to 3
- preact: bfloat16 [512, 24576], P('row', 'col'), may hold values from -8 to 8
- upstream: bfloat16 [512, 24576], P('row', 'col'), may hold values from -3 to 3
Outputs:
- hidden: bfloat16 [512, 24576], P('row', 'col')
- input_grad: bfloat16 [512, 12288], P('col', 'row')
- weight_grad: float32 [12288, 24576], P('row', 'col')
- bias_grad: float32 [24576], P('col')
The draws below stay inside these ranges and needn't reach their ends.
All inputs are finite; a program needn't handle non-finite values.
Results may differ from the reference program's by a relative error of at most 0.0049.
Values may be sent and summed in bfloat16 or wider, within the bound.
A program may use at most 64 MiB of HBM per device.

```python
import math
import jax
import jax.numpy as jnp
from jax import lax

D = 12288
FFW = 24576
TOKENS = 512


def with_spikes(drawn, own_key, source, target, parts, factor):
    def block_of(axis_at):
        return (jnp.arange(drawn.shape[axis_at]) // (drawn.shape[axis_at] // parts)).reshape((-1,) + (1,) * (drawn.ndim - 1 - axis_at))

    near = jax.random.permutation(own_key, parts)[block_of(target)]
    far = (block_of(target) + parts // 2) % parts
    return jnp.where((block_of(source) == near) | (block_of(source) == far), factor * drawn, drawn)


def levels(stream_key, extent, split, least, largest):
    loudness, own = 1.0, jax.random.fold_in(stream_key, 6)
    for axis_at, parts in split:
        steps = jnp.exp(jax.random.uniform(jax.random.fold_in(own, axis_at), (parts,), jnp.float32, least / len(split), largest / len(split)))
        loudness = loudness * jnp.repeat(steps, extent[axis_at] // parts).reshape([-1 if axis == axis_at else 1 for axis in range(len(extent))])
    return loudness


def centred(rng, extent, deviation, most, cuts=(), held_as=jnp.bfloat16):
    result = deviation * jax.random.normal(rng, extent, jnp.float32)
    if cuts:
        result = result * levels(rng, extent, cuts, -0.22, 0.18)
    return jnp.clip(result, -most, most).astype(held_as)


def heavy_noise(rng, shape, width, most, shards, heavy, held_as=jnp.bfloat16):
    drawn = width * jax.random.normal(rng, shape, jnp.float32)
    if shards:
        drawn = drawn * levels(rng, shape, shards, -0.22, 0.18)
    return jnp.clip(with_spikes(drawn, jax.random.fold_in(rng, 3), *heavy), -most, most).astype(held_as)


def setup_inputs(seed: int = 0) -> dict:
    streams_of = jax.random.split(jax.random.key(seed), 7)
    return {
        "tokens_fwd": heavy_noise(streams_of[0], (TOKENS, D), 1.0, 6.0, ((0, 32), (1, 16)), (1, 0, 32, 2.75)),
        "tokens_bwd": centred(streams_of[1], (TOKENS, D), 1.0, 6.0, ((0, 32), (1, 16))),
        "weight": centred(streams_of[2], (D, FFW), D ** -0.5, 0.0546875, ((0, 16), (1, 32))),
        "bias": centred(streams_of[3], (FFW,), 0.5, 3.0, ((0, 32),), jnp.float32),
        "preact": centred(streams_of[4], (TOKENS, FFW), 1.5, 8.0, ((0, 16), (1, 32))),
        "upstream": heavy_noise(streams_of[5], (TOKENS, FFW), 0.5, 3.0, ((0, 16), (1, 32)), (1, 0, 32, 2.75)),
    }


gelu_scale = math.sqrt(2.0 / math.pi)
cubic_term = 0.044715

def gelu_tanh(values):
    inner_arg = gelu_scale * (values + cubic_term * values * values * values)
    return 0.5 * values * (1.0 + jnp.tanh(inner_arg))

def gelu_slope(values):
    tangent = jnp.tanh(gelu_scale * (values + cubic_term * values * values * values))
    return 0.5 * (1.0 + tangent) + 0.5 * values * (1.0 - tangent * tangent) * gelu_scale * (1.0 + 3.0 * cubic_term * values * values)

def reference(tokens_fwd, tokens_bwd, weight, bias, preact, upstream):
    prefwd = jnp.dot(tokens_fwd, weight, preferred_element_type=jnp.float32) + bias
    hidden = gelu_tanh(prefwd).astype(jnp.bfloat16)
    local_grad = (upstream.astype(jnp.float32) * gelu_slope(preact.astype(jnp.float32))).astype(jnp.bfloat16)
    summed = jnp.dot(local_grad, weight.T, preferred_element_type=jnp.float32)
    input_grad = summed.astype(jnp.bfloat16)
    weight_grad = jnp.dot(tokens_bwd.T, local_grad, preferred_element_type=jnp.float32)
    bias_grad = lax.optimization_barrier(jnp.sum(local_grad.astype(jnp.float32), axis=0))
    return (hidden, input_grad, weight_grad, bias_grad)
```

```python
import math

import jax
import jax.numpy as jnp
from jax import lax
from jax.experimental import pallas as pl
from jax.experimental.pallas import tpu as pltpu
from jax.sharding import PartitionSpec as P

gelu_scale = math.sqrt(2.0 / math.pi)
cubic_term = 0.044715
F32, BF16 = jnp.float32, jnp.bfloat16
MESH = pl.DeviceIdType.MESH
TILE = 256


def gelu_tanh(values):
    inner_arg = gelu_scale * (values + cubic_term * values * values * values)
    return 0.5 * values * (1.0 + jnp.tanh(inner_arg))


def gelu_slope(values):
    tangent = jnp.tanh(gelu_scale * (values + cubic_term * values * values * values))
    return 0.5 * (1.0 + tangent) + 0.5 * values * (1.0 - tangent * tangent) * gelu_scale * (
        1.0 + 3.0 * cubic_term * values * values
    )


def flip(i, k):
    if k == 1:
        return i + 1 - 2 * lax.rem(i, 2)
    if k == 2:
        return lax.rem(i + 2, 4)
    return 3 - i


class Sems:
    def __init__(self, send, recv):
        self.send, self.recv, self.n = send, recv, 0

    def pair(self):
        self.n += 1
        return self.send.at[self.n - 1], self.recv.at[self.n - 1]


N_LOCAL = 6
N_REMOTE = 80


def kernel(
    fwd_hbm, bwd_hbm, w_hbm, bias_hbm, pre_hbm, up_hbm,
    hidden_ref, igrad_ref, wgrad_ref, bgrad_ref,
    xf, xb, g, q, w, bias, pre, up,
    half, core_out, core_in, x_out, x_in, y_out, y_in,
    rs_out, rs_in, line_out, line_in, sums,
    local_sem, send_sem, recv_sem,
):
    row, col = lax.axis_index("row"), lax.axis_index("col")
    yh, x, core = row // 8, lax.rem(row // 2, 4), lax.rem(row, 2)
    yl, z = col // 8, lax.rem(col, 8)
    early = yl // 2

    def device(yh=yh, x=x, core=core, yl=yl, z=z):
        return (yh * 8 + x * 2 + core, yl * 8 + z)

    up_z, down_z = lax.rem(z + 1, 8), lax.rem(z + 7, 8)
    near_z = (device(z=up_z), device(z=down_z))
    near_x = [device(x=flip(x, k)) for k in (1, 2, 3)]
    near_y = [device(yl=flip(yl, k)) for k in (1, 2, 3)]
    far_y = device(yh=1 - yh)
    twin = device(core=1 - core)
    partners = [*near_z, *near_x, *near_y, far_y, twin]

    sems = Sems(send_sem, recv_sem)
    started = []

    def copy(src, dst, target):
        s, r = sems.pair()
        c = pltpu.make_async_remote_copy(
            src_ref=src, dst_ref=dst, send_sem=s, recv_sem=r,
            device_id=target, device_id_type=MESH,
        )
        started.append(c)
        return c

    def at_z(ref, pair, at):
        return ref.at[pl.ds(2 * pair, 2), at // 4, lax.rem(at // 2, 2), lax.rem(at, 2)]

    def own(ref):
        return ref.at[yl, z // 4, lax.rem(z // 2, 2), lax.rem(z, 2)]

    def from_y(ref, at):
        return ref.at[at, z // 4, lax.rem(z // 2, 2), lax.rem(z, 2)]

    loads = [
        pltpu.make_async_copy(src, dst, local_sem.at[i])
        for i, (src, dst) in enumerate(
            [(fwd_hbm, own(xf)), (pre_hbm, pre), (up_hbm, up), (bwd_hbm, own(xb)), (w_hbm, w), (bias_hbm, bias)]
        )
    ]
    for c in loads:
        c.start()
    barrier = pltpu.get_barrier_semaphore()
    for d in partners:
        pl.semaphore_signal(barrier, inc=1, device_id=d, device_id_type=MESH)
    for c in loads[:4]:
        c.wait()
    grad = (up[...].astype(F32) * gelu_slope(pre[...].astype(F32))).astype(BF16)
    g[yh, x, core] = grad
    pl.semaphore_wait(barrier, len(partners))

    def line(ref):
        return [copy(own(ref), own(ref), near_y[k - 1]) for k in (1, 2, 3)]

    f_line = line(xf)
    for c in f_line:
        c.start()
    g_far = copy(g.at[yh, x, core], g.at[yh, x, core], far_y)
    g_far.start()
    g_x = [copy(g.at[yh, x, core], g.at[yh, x, core], d) for d in near_x]
    for c in g_x:
        c.start()
    b_line = line(xb)
    for c in b_line:
        c.start()

    class Ring:
        def __init__(self, ref):
            self.ref = ref
            self.pairs = (early, 1 - early)
            self.hops = ((4, 3), (3, 4))
            self.sent = {}

        def step(self, s, which):
            for way in (0, 1):
                if s >= self.hops[which][way]:
                    continue
                if s > 0:
                    self.sent[s - 1, which, way].wait_recv()
                source = lax.rem(z - s + 8, 8) if way == 0 else lax.rem(z + s, 8)
                block = at_z(self.ref, self.pairs[which], source)
                c = copy(block, block, near_z[way])
                c.start()
                self.sent[s, which, way] = c

        def finish(self):
            for which in (0, 1):
                for way in (0, 1):
                    self.sent[self.hops[which][way] - 1, which, way].wait_recv()

    f_ring, b_ring = Ring(xf), Ring(xb)
    f_line[0].wait_recv()
    f_ring.step(0, 0)
    f_line[1].wait_recv()
    f_line[2].wait_recv()
    f_ring.step(0, 1)
    f_ring.step(1, 0)
    f_ring.step(1, 1)
    for c in g_x:
        c.wait_recv()
    g_twin = [copy(g.at[yh, :, core], g.at[yh, :, core], twin)]
    g_twin[0].start()
    g_far.wait_recv()
    g_x2 = [copy(g.at[1 - yh, x, core], g.at[1 - yh, x, core], d) for d in near_x]
    for c in g_x2:
        c.start()
    f_ring.step(2, 0)
    f_ring.step(2, 1)
    f_ring.step(3, 0)
    f_ring.step(3, 1)
    for c in b_line:
        c.wait_recv()
    b_ring.step(0, 0)
    b_ring.step(0, 1)
    for c in g_x2:
        c.wait_recv()
    g_twin.append(copy(g.at[1 - yh, :, core], g.at[1 - yh, :, core], twin))
    g_twin[1].start()
    loads[4].wait()
    loads[5].wait()

    f_ring.finish()

    def forward_half(which, store):
        lhs = xf[:, :, which].reshape(256, 768)

        def body(n, carry):
            at = pl.ds(pl.multiple_of(n * TILE, TILE), TILE)
            store(at, jnp.dot(lhs, w[:, at], preferred_element_type=F32).reshape(2, 4, 32, TILE))
            return carry

        lax.fori_loop(0, 3, body, 0)

    def store_out(at, value):
        core_out[:, :, :, at] = value.astype(BF16)

    def store_half(at, value):
        half[:, :, :, at] = value

    forward_half(1 - core, store_out)
    c_twin = copy(core_out, core_in, twin)
    c_twin.start()

    for c in g_twin:
        c.wait_recv()

    def q_body(n, carry):
        at = pl.ds(pl.multiple_of(n * TILE, TILE), TILE)
        q[:, :, :, at] = lax.dot_general(
            g[...].reshape(512, 768), w[at, :], (((1,), (1,)), ((), ())), preferred_element_type=F32
        ).reshape(4, 8, 16, TILE)
        return carry

    lax.fori_loop(0, 3, q_body, 0)

    rs_hops = ((4, 3), (3, 4))
    rs_sent = {}
    slot_of = {}
    for pair in (0, 1):
        for way in (0, 1):
            for s in range(rs_hops[pair][way]):
                slot_of[s, pair, way] = len(slot_of)

    def rs_step(s, pair):
        for way in (0, 1):
            hops = rs_hops[pair][way]
            if s >= hops:
                continue
            left = hops - s
            target = lax.rem(z + left, 8) if way == 0 else lax.rem(z - left + 8, 8)
            value = q[pl.ds(2 * pair, 2), target]
            if s > 0:
                before = rs_sent[s - 1, pair, way]
                before.wait_recv()
                value = value + rs_in[slot_of[s - 1, pair, way]].astype(F32)
            slot = slot_of[s, pair, way]
            rs_out[slot] = value.astype(BF16)
            c = copy(rs_out.at[slot], rs_in.at[slot], near_z[way])
            c.start()
            rs_sent[s, pair, way] = c

    rs_step(0, 0)
    rs_step(0, 1)
    forward_half(core, store_half)
    b_ring.step(1, 0)
    b_ring.step(1, 1)
    c_twin.wait_recv()
    half[...] = half[...] + core_in[...].astype(F32)
    x_copies = []
    for k in (1, 2, 3):
        x_out[k - 1] = half[:, flip(x, k)].astype(BF16)
        c = copy(x_out.at[k - 1], x_in.at[k - 1], near_x[k - 1])
        c.start()
        x_copies.append(c)
    rs_step(1, 0)
    rs_step(1, 1)
    bgrad_ref[...] = jnp.sum(g[...].reshape(512, 768).astype(F32), axis=0, keepdims=True)
    b_ring.step(2, 0)
    b_ring.step(2, 1)
    rs_step(2, 0)
    rs_step(2, 1)
    for c in x_copies:
        c.wait_recv()
    sums[...] = half[:, x] + x_in[0].astype(F32) + x_in[1].astype(F32) + x_in[2].astype(F32)
    y_out[...] = sums[1 - yh].astype(BF16)
    c_far = copy(y_out, y_in, far_y)
    c_far.start()
    b_ring.step(3, 0)
    b_ring.step(3, 1)
    rs_step(3, 0)
    rs_step(3, 1)

    for pair in (0, 1):
        value = q[pl.ds(2 * pair, 2), z]
        for way in (0, 1):
            s = rs_hops[pair][way] - 1
            rs_sent[s, pair, way].wait_recv()
            value = value + rs_in[slot_of[s, pair, way]].astype(F32)
        q[pl.ds(2 * pair, 2), z] = value
    l_copies = []
    for k in (1, 2, 3):
        line_out[k - 1] = q[flip(yl, k), z].astype(BF16)
        c = copy(line_out.at[k - 1], line_in.at[k - 1], near_y[k - 1])
        c.start()
        l_copies.append(c)

    c_far.wait_recv()
    hidden_ref[...] = gelu_tanh(sums[yh] + y_in[...].astype(F32) + bias[...]).astype(BF16)

    b_ring.finish()

    def w_body(n, carry):
        at = pl.ds(pl.multiple_of(n * TILE, TILE), TILE)
        wgrad_ref[at, :] = lax.dot_general(
            xb[:, :, :, :, :, at].reshape(512, TILE), g[...].reshape(512, 768), (((0,), (0,)), ((), ())),
            preferred_element_type=F32,
        )
        return carry

    lax.fori_loop(0, 3, w_body, 0)

    for c in l_copies:
        c.wait_recv()
    igrad_ref[...] = (
        q[yl, z] + line_in[0].astype(F32) + line_in[1].astype(F32) + line_in[2].astype(F32)
    ).astype(BF16)
    for c in started:
        c.wait_send()


def local(tokens_fwd, tokens_bwd, weight, bias, preact, upstream):
    any_space = pl.BlockSpec(memory_space=pl.ANY)
    vmem = pl.BlockSpec(memory_space=pltpu.VMEM)
    hidden, input_grad, weight_grad, bias_grad = pl.pallas_call(
        kernel,
        out_shape=(
            jax.ShapeDtypeStruct((32, 768), BF16),
            jax.ShapeDtypeStruct((16, 768), BF16),
            jax.ShapeDtypeStruct((768, 768), F32),
            jax.ShapeDtypeStruct((1, 768), F32),
        ),
        in_specs=[any_space] * 6,
        out_specs=[vmem] * 4,
        scratch_shapes=[
            pltpu.VMEM((4, 2, 2, 2, 16, 768), BF16),
            pltpu.VMEM((4, 2, 2, 2, 16, 768), BF16),
            pltpu.VMEM((2, 4, 2, 32, 768), BF16),
            pltpu.VMEM((4, 8, 16, 768), F32),
            pltpu.VMEM((768, 768), BF16),
            pltpu.VMEM((1, 768), F32),
            pltpu.VMEM((32, 768), BF16),
            pltpu.VMEM((32, 768), BF16),
            pltpu.VMEM((2, 4, 32, 768), F32),
            pltpu.VMEM((2, 4, 32, 768), BF16),
            pltpu.VMEM((2, 4, 32, 768), BF16),
            pltpu.VMEM((3, 2, 32, 768), BF16),
            pltpu.VMEM((3, 2, 32, 768), BF16),
            pltpu.VMEM((32, 768), BF16),
            pltpu.VMEM((32, 768), BF16),
            pltpu.VMEM((14, 2, 16, 768), BF16),
            pltpu.VMEM((14, 2, 16, 768), BF16),
            pltpu.VMEM((3, 16, 768), BF16),
            pltpu.VMEM((3, 16, 768), BF16),
            pltpu.VMEM((2, 32, 768), F32),
            pltpu.SemaphoreType.DMA((N_LOCAL,)),
            pltpu.SemaphoreType.DMA((N_REMOTE,)),
            pltpu.SemaphoreType.DMA((N_REMOTE,)),
        ],
        compiler_params=pltpu.CompilerParams(
            collective_id=0, has_side_effects=True, vmem_limit_bytes=48 * 2**20
        ),
        cost_estimate=pl.CostEstimate(flops=3 * 2 * 512 * 768 * 768, bytes_accessed=8 * 2**20, transcendentals=50000),
        name="feed_forward",
    )(tokens_fwd, tokens_bwd, weight, bias.reshape(1, 768), preact, upstream)
    return hidden, input_grad, weight_grad, bias_grad.reshape(768)


def solution(mesh):
    return jax.shard_map(
        local,
        mesh=mesh,
        in_specs=(
            P("col", "row"),
            P("col", "row"),
            P("row", "col"),
            P("col"),
            P("row", "col"),
            P("row", "col"),
        ),
        out_specs=(P("row", "col"), P("col", "row"), P("row", "col"), P("col")),
        check_vma=False,
    )
```

```python
import math

import jax
import jax.numpy as jnp
from jax import lax
from jax.experimental import pallas as pl
from jax.experimental.pallas import tpu as pltpu
from jax.sharding import PartitionSpec as P

gelu_scale = math.sqrt(2.0 / math.pi)
cubic_term = 0.044715
F32, BF16 = jnp.float32, jnp.bfloat16
MESH = pl.DeviceIdType.MESH
TILE = 256


def gelu_tanh(values):
    inner_arg = gelu_scale * (values + cubic_term * values * values * values)
    return 0.5 * values * (1.0 + jnp.tanh(inner_arg))


def gelu_slope(values):
    tangent = jnp.tanh(gelu_scale * (values + cubic_term * values * values * values))
    return 0.5 * (1.0 + tangent) + 0.5 * values * (1.0 - tangent * tangent) * gelu_scale * (
        1.0 + 3.0 * cubic_term * values * values
    )


def flip(i, k):
    if k == 1:
        return i + 1 - 2 * lax.rem(i, 2)
    if k == 2:
        return lax.rem(i + 2, 4)
    return 3 - i


class Sems:
    def __init__(self, send, recv):
        self.send, self.recv, self.n = send, recv, 0

    def pair(self):
        self.n += 1
        return self.send.at[self.n - 1], self.recv.at[self.n - 1]


N_LOCAL = 6
N_REMOTE = 96


def kernel(
    fwd_hbm, bwd_hbm, w_hbm, bias_hbm, pre_hbm, up_hbm,
    hidden_ref, igrad_ref, wgrad_ref, bgrad_ref,
    xf, xb, g, q, w, bias, pre, up,
    p, core_out, core_in, x_out, x_in, y_out, y_in,
    rs_out, rs_in, line_out, line_in, sums,
    local_sem, send_sem, recv_sem,
):
    row, col = lax.axis_index("row"), lax.axis_index("col")
    yh, x, core = row // 8, lax.rem(row // 2, 4), lax.rem(row, 2)
    yl, z = col // 8, lax.rem(col, 8)
    mate, opposite = flip(yl, 1), 1 - yl // 2

    def device(yh=yh, x=x, core=core, yl=yl, z=z):
        return (yh * 8 + x * 2 + core, yl * 8 + z)

    near_z = (device(z=lax.rem(z + 1, 8)), device(z=lax.rem(z + 7, 8)))
    near_x = [device(x=flip(x, k)) for k in (1, 2, 3)]
    near_y = [device(yl=flip(yl, k)) for k in (1, 2, 3)]
    far_y = device(yh=1 - yh)
    twin = device(core=1 - core)
    near_row = [*near_x, twin, *[device(x=flip(x, k), core=1 - core) for k in (1, 2, 3)]]
    partners = [*near_z, *near_y, far_y, *near_row]

    sems = Sems(send_sem, recv_sem)
    started = []

    def copy(src, dst, target):
        s, r = sems.pair()
        c = pltpu.make_async_remote_copy(
            src_ref=src, dst_ref=dst, send_sem=s, recv_sem=r,
            device_id=target, device_id_type=MESH,
        )
        started.append(c)
        c.start()
        return c

    def at_z(at):
        return at // 4, lax.rem(at // 2, 2), lax.rem(at, 2)

    loads = [
        pltpu.make_async_copy(src, dst, local_sem.at[i])
        for i, (src, dst) in enumerate(
            [
                (fwd_hbm, xf.at[(yl, *at_z(z))]), (pre_hbm, pre), (up_hbm, up), (w_hbm, w),
                (bwd_hbm, xb.at[(yl, *at_z(z))]), (bias_hbm, bias),
            ]
        )
    ]
    barrier = pltpu.get_barrier_semaphore()
    for d in partners:
        pl.semaphore_signal(barrier, inc=1, device_id=d, device_id_type=MESH)
    for c in loads:
        c.start()
    pl.semaphore_wait(barrier, len(partners))

    class Gather:
        def __init__(self, hbm, ref):
            self.hbm, self.ref = hbm, ref
            self.hops = ((4, 3), (3, 4), (4, 3)) if ref is xf else ((3, 4), (4, 3), (3, 4))
            self.sent = {}

        def line(self):
            block = self.ref.at[(yl, *at_z(z))]
            self.lines = [copy(self.hbm, block, d) for d in near_y]

        def chunk(self, which, at):
            rows = (pl.ds(yl, 1), pl.ds(mate, 1), pl.ds(2 * opposite, 2))[which]
            return self.ref.at[(rows, *at_z(at))]

        def step(self, s, which):
            if s == 0 and which == 1:
                self.lines[0].wait_recv()
            if s == 0 and which == 2:
                self.lines[1].wait_recv()
                self.lines[2].wait_recv()
            for way in (0, 1):
                if s >= self.hops[which][way]:
                    continue
                if s > 0:
                    self.sent[s - 1, which, way].wait_recv()
                source = lax.rem(z - s + 8, 8) if way == 0 else lax.rem(z + s, 8)
                block = self.chunk(which, source)
                if s == 0 and which == 0:
                    src = self.hbm
                    block = self.ref.at[(yl, *at_z(z))]
                else:
                    src = block
                self.sent[s, which, way] = copy(src, block, near_z[way])

        def finish(self):
            for which in (0, 1, 2):
                for way in (0, 1):
                    self.sent[self.hops[which][way] - 1, which, way].wait_recv()

    fwd, bwd = Gather(fwd_hbm, xf), Gather(bwd_hbm, xb)

    def gather_grad():
        grad = (up[...].astype(F32) * gelu_slope(pre[...].astype(F32))).astype(BF16)
        g[yh, x, core] = grad

    def spread_grad(at):
        return [copy(g.at[at, x, core], g.at[at, x, core], d) for d in near_row]

    rs_hops = ((4, 3), (3, 4))
    rs_sent = {}
    slot_of = {}
    for part in (0, 1):
        for way in (0, 1):
            for s in range(rs_hops[part][way]):
                slot_of[s, part, way] = len(slot_of)
    halves = (yh, 1 - yh)

    def back_half(part):
        j = halves[part]
        rows = g[j].reshape(256, 768)

        def body(n, carry):
            at = pl.ds(pl.multiple_of(n * TILE, TILE), TILE)
            q[pl.ds(2 * j, 2), :, :, at] = lax.dot_general(
                rows, w[at, :], (((1,), (1,)), ((), ())), preferred_element_type=F32
            ).reshape(2, 8, 16, TILE)
            return carry

        lax.fori_loop(0, 3, body, 0)

    def rs_step(s, part):
        for way in (0, 1):
            hops = rs_hops[part][way]
            if s >= hops:
                continue
            left = hops - s
            target = lax.rem(z + left, 8) if way == 0 else lax.rem(z - left + 8, 8)
            value = q[pl.ds(2 * halves[part], 2), target]
            if s > 0:
                rs_sent[s - 1, part, way].wait_recv()
                value = value + rs_in[slot_of[s - 1, part, way]].astype(F32)
            slot = slot_of[s, part, way]
            rs_out[slot] = value.astype(BF16)
            rs_sent[s, part, way] = copy(rs_out.at[slot], rs_in.at[slot], near_z[way])

    def rs_end(part):
        value = q[pl.ds(2 * halves[part], 2), z]
        for way in (0, 1):
            s = rs_hops[part][way] - 1
            rs_sent[s, part, way].wait_recv()
            value = value + rs_in[slot_of[s, part, way]].astype(F32)
        q[pl.ds(2 * halves[part], 2), z] = value

    f_halves = (1 - yh, yh)

    def forward_half(part):
        j = f_halves[part]
        rows = xf[pl.ds(2 * j, 2)].reshape(256, 768)

        def body(n, carry):
            at = pl.ds(pl.multiple_of(n * TILE, TILE), TILE)
            p[part, :, :, :, at] = jnp.dot(rows, w[:, at], preferred_element_type=F32).reshape(4, 2, 32, TILE)
            return carry

        lax.fori_loop(0, 3, body, 0)
        core_out[part] = p[part, :, 1 - core].astype(BF16)
        return copy(core_out.at[part], core_in.at[part], twin)

    def forward_x(part, from_twin):
        from_twin.wait_recv()
        copies = []
        for k in (1, 2, 3):
            there = flip(x, k)
            x_out[part, k - 1] = (p[part, there, core] + core_in[part, there].astype(F32)).astype(BF16)
            copies.append(copy(x_out.at[part, k - 1], x_in.at[part, k - 1], near_x[k - 1]))
        sums[part] = p[part, x, core] + core_in[part, x].astype(F32)
        return copies

    def forward_sum(part, copies):
        for c in copies:
            c.wait_recv()
        return sums[part] + x_in[part, 0].astype(F32) + x_in[part, 1].astype(F32) + x_in[part, 2].astype(F32)

    fwd.line()
    fwd.step(0, 0)
    bwd.line()
    loads[1].wait()
    loads[2].wait()
    gather_grad()
    g_far = copy(g.at[yh, x, core], g.at[yh, x, core], far_y)
    g_here = spread_grad(yh)
    bwd.step(0, 0)
    fwd.step(1, 0)
    fwd.step(0, 1)
    fwd.step(0, 2)
    loads[3].wait()
    for c in g_here:
        c.wait_recv()
    back_half(0)
    rs_step(0, 0)
    fwd.step(2, 0)
    fwd.step(1, 1)
    fwd.step(1, 2)
    g_far.wait_recv()
    g_there = spread_grad(1 - yh)
    fwd.step(3, 0)
    rs_step(1, 0)
    fwd.step(2, 1)
    fwd.step(2, 2)
    bwd.step(1, 0)
    bwd.step(0, 1)
    bwd.step(0, 2)
    for c in g_there:
        c.wait_recv()
    back_half(1)
    rs_step(0, 1)
    fwd.step(3, 1)
    fwd.step(3, 2)
    rs_step(2, 0)
    bwd.step(2, 0)
    for c in loads:
        if c is not loads[1] and c is not loads[2] and c is not loads[3]:
            c.wait()
    fwd.finish()
    twin_0 = forward_half(0)
    rs_step(1, 1)
    bwd.step(1, 1)
    bwd.step(1, 2)
    twin_1 = forward_half(1)
    x_0 = forward_x(0, twin_0)
    rs_step(3, 0)
    bwd.step(3, 0)
    x_1 = forward_x(1, twin_1)
    rs_step(2, 1)
    bwd.step(2, 1)
    bwd.step(2, 2)
    y_out[...] = forward_sum(0, x_0).astype(BF16)
    far = copy(y_out, y_in, far_y)
    rs_end(0)
    bgrad_ref[...] = jnp.sum(g[...].reshape(512, 768).astype(F32), axis=0)
    rs_step(3, 1)
    bwd.step(3, 1)
    bwd.step(3, 2)
    sums[1] = forward_sum(1, x_1)
    rs_end(1)
    l_copies = []
    for k in (1, 2, 3):
        line_out[k - 1] = q[flip(yl, k), z].astype(BF16)
        l_copies.append(copy(line_out.at[k - 1], line_in.at[k - 1], near_y[k - 1]))
    bwd.finish()

    def w_body(n, carry):
        at = pl.ds(pl.multiple_of(n * TILE, TILE), TILE)
        wgrad_ref[at, :] = lax.dot_general(
            xb[:, :, :, :, :, at].reshape(512, TILE), g[...].reshape(512, 768), (((0,), (0,)), ((), ())),
            preferred_element_type=F32,
        )
        return carry

    lax.fori_loop(0, 3, w_body, 0)

    far.wait_recv()
    hidden_ref[...] = gelu_tanh(sums[1] + y_in[...].astype(F32) + bias[...]).astype(BF16)
    for c in l_copies:
        c.wait_recv()
    igrad_ref[...] = (
        q[yl, z] + line_in[0].astype(F32) + line_in[1].astype(F32) + line_in[2].astype(F32)
    ).astype(BF16)
    for c in started:
        c.wait_send()


def local(tokens_fwd, tokens_bwd, weight, bias, preact, upstream):
    hbm = pl.BlockSpec(memory_space=pltpu.HBM)
    vmem = pl.BlockSpec(memory_space=pltpu.VMEM)
    shapes = (
        jax.ShapeDtypeStruct((32, 768), BF16),
        jax.ShapeDtypeStruct((16, 768), BF16),
        jax.ShapeDtypeStruct((768, 768), F32),
        jax.ShapeDtypeStruct((768,), F32),
    )
    tokens_fwd, tokens_bwd, weight, bias, preact, upstream = [
        pltpu.with_memory_space_constraint(a, pltpu.HBM)
        for a in (tokens_fwd, tokens_bwd, weight, bias, preact, upstream)
    ]
    return pl.pallas_call(
        kernel,
        out_shape=shapes,
        in_specs=[hbm] * 6,
        out_specs=[vmem] * 4,
        scratch_shapes=[
            pltpu.VMEM((4, 2, 2, 2, 16, 768), BF16),
            pltpu.VMEM((4, 2, 2, 2, 16, 768), BF16),
            pltpu.VMEM((2, 4, 2, 32, 768), BF16),
            pltpu.VMEM((4, 8, 16, 768), F32),
            pltpu.VMEM((768, 768), BF16),
            pltpu.VMEM((768,), F32),
            pltpu.VMEM((32, 768), BF16),
            pltpu.VMEM((32, 768), BF16),
            pltpu.VMEM((2, 4, 2, 32, 768), F32),
            pltpu.VMEM((2, 4, 32, 768), BF16),
            pltpu.VMEM((2, 4, 32, 768), BF16),
            pltpu.VMEM((2, 3, 32, 768), BF16),
            pltpu.VMEM((2, 3, 32, 768), BF16),
            pltpu.VMEM((32, 768), BF16),
            pltpu.VMEM((32, 768), BF16),
            pltpu.VMEM((14, 2, 16, 768), BF16),
            pltpu.VMEM((14, 2, 16, 768), BF16),
            pltpu.VMEM((3, 16, 768), BF16),
            pltpu.VMEM((3, 16, 768), BF16),
            pltpu.VMEM((2, 32, 768), F32),
            pltpu.SemaphoreType.DMA((N_LOCAL,)),
            pltpu.SemaphoreType.DMA((N_REMOTE,)),
            pltpu.SemaphoreType.DMA((N_REMOTE,)),
        ],
        compiler_params=pltpu.CompilerParams(
            collective_id=0, has_side_effects=True, vmem_limit_bytes=48 * 2**20
        ),
        cost_estimate=pl.CostEstimate(flops=3 * 2 * 512 * 768 * 768, bytes_accessed=8 * 2**20, transcendentals=50000),
        name="feed_forward",
    )(tokens_fwd, tokens_bwd, weight, bias, preact, upstream)

def solution(mesh):
    return jax.shard_map(
        local,
        mesh=mesh,
        in_specs=(
            P("col", "row"),
            P("col", "row"),
            P("row", "col"),
            P("col"),
            P("row", "col"),
            P("row", "col"),
        ),
        out_specs=(P("row", "col"), P("col", "row"), P("row", "col"), P("col")),
        check_vma=False,
    )
```

```python
import math

import jax
import jax.numpy as jnp
from jax import lax
from jax.experimental import pallas as pl
from jax.experimental.pallas import tpu as pltpu
from jax.sharding import PartitionSpec as P

gelu_scale = math.sqrt(2.0 / math.pi)
cubic_term = 0.044715
F32, BF16 = jnp.float32, jnp.bfloat16
MESH = pl.DeviceIdType.MESH
TILE = 256


def gelu_tanh(values):
    inner_arg = gelu_scale * (values + cubic_term * values * values * values)
    return 0.5 * values * (1.0 + jnp.tanh(inner_arg))


def gelu_slope(values):
    tangent = jnp.tanh(gelu_scale * (values + cubic_term * values * values * values))
    return 0.5 * (1.0 + tangent) + 0.5 * values * (1.0 - tangent * tangent) * gelu_scale * (
        1.0 + 3.0 * cubic_term * values * values
    )


def flip(i, k):
    if k == 1:
        return i + 1 - 2 * lax.rem(i, 2)
    if k == 2:
        return lax.rem(i + 2, 4)
    return 3 - i


class Sems:
    def __init__(self, send, recv):
        self.send, self.recv, self.n = send, recv, 0

    def pair(self):
        self.n += 1
        return self.send.at[self.n - 1], self.recv.at[self.n - 1]


ORDER = (
    ("b", 0, 0, 0), ("f", "line"), ("f", 0, 0, 0), ("far",), ("f", 0, 1, 0), ("spread", 0), ("b", 1, 0, 0),
    ("b", 1, 0, 1), ("f", 0, 2, 0), ("f", 1, 1, 1), ("f", 1, 0, 1), ("spread", 1), ("b", "line"), ("f", 1, 1, 0),
    ("f", 1, 0, 0), ("f", 1, 2, 1), ("f", 1, 2, 0), ("back", 0), ("rs", 0, 0, 1), ("rs", 0, 0, 0), ("back", 1),
    ("rs", 0, 1, 0), ("rs", 0, 1, 1), ("fwd", 0), ("rs", 1, 0, 1), ("rs", 1, 0, 0), ("rs", 1, 1, 0), ("rs", 1, 1, 1),
    ("fwd", 1), ("fsum", 0), ("rsend", 0), ("rsend", 1), ("rsline",), ("wg",), ("fsum", 1), ("bg",), ("hid",),
    ("igrad",),
)

RS_SLOT = {"three": 0, "four": 2, "one": 3, "two": 5}
RS_SIZE = {"three": 2, "four": 1, "one": 2, "two": 2}
N_LOCAL = 6
N_REMOTE = 112


def kernel(
    fwd_hbm, bwd_hbm, w_hbm, bias_hbm, pre_hbm, up_hbm,
    hidden_ref, igrad_ref, wgrad_ref, bgrad_ref,
    xf, xb, g, q, w, bias, pre, up,
    p, x_out, x_in, y_out, y_in,
    rs_out, rs_in, line_out, line_in, sums,
    local_sem, send_sem, recv_sem,
):
    row, col = lax.axis_index("row"), lax.axis_index("col")
    yh, x, core = row // 8, lax.rem(row // 2, 4), lax.rem(row, 2)
    yl, z = col // 8, lax.rem(col, 8)
    mate, opposite = flip(yl, 1), 1 - yl // 2

    def device(yh=yh, x=x, core=core, yl=yl, z=z):
        return (yh * 8 + x * 2 + core, yl * 8 + z)

    along_z = {away: device(z=lax.rem(z + away + 8, 8)) for away in (1, -1, 2, -2)}
    near_z = (along_z[1], along_z[-1])
    near_y = [device(yl=flip(yl, k)) for k in (1, 2, 3)]
    far_y = device(yh=1 - yh)
    row_places = [(flip(x, k) if k else x, c) for k, c in ((2, 1 - core), (2, core), (1, 1 - core), (3, 1 - core), (1, core), (3, core), (0, 1 - core))]
    near_row = [device(x=there, core=c) for there, c in row_places]
    partners = [*along_z.values(), *near_y, far_y, *near_row]

    sems = Sems(send_sem, recv_sem)
    started = []

    def copy(src, dst, target):
        s, r = sems.pair()
        c = pltpu.make_async_remote_copy(
            src_ref=src, dst_ref=dst, send_sem=s, recv_sem=r,
            device_id=target, device_id_type=MESH,
        )
        started.append(c)
        c.start()
        return c

    def at_z(at):
        return at // 4, lax.rem(at // 2, 2), lax.rem(at, 2)

    loads = [
        pltpu.make_async_copy(src, dst, local_sem.at[i])
        for i, (src, dst) in enumerate(
            [
                (fwd_hbm, xf.at[(yl, *at_z(z))]), (pre_hbm, pre), (up_hbm, up), (w_hbm, w),
                (bwd_hbm, xb.at[(yl, *at_z(z))]), (bias_hbm, bias),
            ]
        )
    ]
    barrier = pltpu.get_barrier_semaphore()
    for d in partners:
        pl.semaphore_signal(barrier, inc=1, device_id=d, device_id_type=MESH)
    for c in loads:
        c.start()
    loads[1].wait()
    loads[2].wait()
    g[yh, x, core] = (up[...].astype(F32) * gelu_slope(pre[...].astype(F32))).astype(BF16)
    pl.semaphore_wait(barrier, len(partners))

    waited = {1, 2}

    def arrived(*copies):
        for c in copies:
            if id(c) not in waited:
                waited.add(id(c))
                c.wait_recv()

    def loaded(*which):
        for i in which:
            if i not in waited:
                waited.add(i)
                loads[i].wait()

    class Gather:
        def __init__(self, hbm, ref, hops, two, z_first=False):
            self.hbm, self.ref, self.hops, self.two, self.z_first = hbm, ref, hops, two, z_first
            self.sent = {}

        def line(self):
            if self.z_first:
                arrived(*self.sent.values())
                loaded(4)
                block = self.ref.at[yl]
                self.lines = [copy(block, block, d) for d in near_y]
                return
            block = self.ref.at[(yl, *at_z(z))]
            self.lines = [copy(self.hbm, block, d) for d in near_y]

        def first(self, which):
            return [(self.lines[0],), self.lines[1:]][which - 1] if which else ()

        def near(self, which):
            arrived(*self.first(which))
            block = self.block(which, z)
            src = self.hbm if which == 0 else block
            for away in (2, 1):
                for way in (0, 1):
                    self.sent[away, which, way] = copy(src, block, along_z[(away, -away)[way]])

        def far(self, which, way):
            arrived(self.sent[2, which, way])
            sign = (1, -1)[way]
            source = lax.rem(z - 2 * sign + 8, 8)
            if which == 2:
                half = self.ref.at[(2 * opposite + way, *at_z(source))]
                self.sent[4, which, way] = copy(half, half, along_z[2 * sign])
            elif which == way:
                block = self.block(which, source)
                self.sent[4, which, way] = copy(block, block, along_z[2 * sign])
            block = self.block(which, source)
            self.sent[3, which, way] = copy(block, block, along_z[sign])

        def block(self, which, source):
            if which == 0:
                return self.ref.at[(yl, *at_z(source))]
            rows = pl.ds(mate, 1) if which == 1 else pl.ds(2 * opposite, 2)
            return self.ref.at[(rows, *at_z(source))]

        def step(self, s, which, way):
            if self.two:
                return self.far(which, way) if s else self.near(which)
            source = lax.rem(z - s + 8, 8) if way == 0 else lax.rem(z + s, 8)
            if which == 0:
                block = self.ref.at[(yl, *at_z(source))]
            else:
                rows = pl.ds(mate, 1) if which == 1 else pl.ds(2 * opposite, 2)
                block = self.ref.at[(rows, *at_z(source))]
            if s > 0:
                arrived(self.sent[s - 1, which, way])
            elif which == 1:
                arrived(self.lines[0])
            elif which == 2:
                arrived(*self.lines[1:])
            src = self.hbm if s == 0 and which == 0 else block
            self.sent[s, which, way] = copy(src, block, near_z[way])

        def finish(self):
            if self.z_first:
                arrived(*self.lines)
                return
            if self.two:
                arrived(*self.sent.values())
                return
            for which in (0, 1, 2):
                for way in (0, 1):
                    arrived(self.sent[self.hops[which][way] - 1, which, way])

    gathers = {
        "f": Gather(fwd_hbm, xf, ((4, 3), (3, 4), (4, 3)), True),
        "b": Gather(bwd_hbm, xb, ((3, 4), (4, 3), (3, 4)), True, True),
    }
    sent = {}

    def far():
        sent["far"] = copy(g.at[yh, x, core], g.at[yh, x, core], far_y)

    def spread(half):
        if half == 1:
            arrived(sent["far"])
        at = (yh, 1 - yh)[half]
        sent["spread", half] = [copy(g.at[at, x, core], g.at[at, x, core], d) for d in near_row]

    halves = (yh, 1 - yh)

    def back(part):
        arrived(*sent["spread", part])
        loaded(3)
        j = halves[part]
        rows = g[j].reshape(256, 768)

        def body(n, carry):
            at = pl.ds(pl.multiple_of(n * TILE, TILE), TILE)
            q[pl.ds(2 * j, 2), :, :, at] = lax.dot_general(
                rows, w[at, :], (((1,), (1,)), ((), ())), preferred_element_type=F32
            ).reshape(2, 8, 16, TILE)
            return carry

        lax.fori_loop(0, 3, body, 0)

    def rs_send(name, part, way, value, away):
        slots = pl.ds(RS_SLOT[name] + 7 * (2 * part + way), value.shape[0])
        rs_out[slots] = value.astype(BF16)
        sent[name, part, way] = copy(rs_out.at[slots], rs_in.at[slots], along_z[away])

    def rs_got(name, part, way):
        arrived(sent[name, part, way])
        slots = pl.ds(RS_SLOT[name] + 7 * (2 * part + way), RS_SIZE[name])
        return rs_in[slots].astype(F32)

    def rs(s, part, way):
        j, sign = halves[part], (1, -1)[way]

        def sums_for(away):
            return q[pl.ds(2 * j, 2), lax.rem(z + sign * away + 8, 8)]

        if s == 0:
            rs_send("three", part, way, sums_for(3), sign)
            rs_send("four", part, way, q[pl.ds(2 * j + way, 1), lax.rem(z + 4, 8)], 2 * sign)
            rs_send("one", part, way, sums_for(1), sign)
        else:
            value = sums_for(2) + rs_got("three", part, way)
            more = rs_got("four", part, way)
            parts = [value[:1] + more, value[1:]] if way == 0 else [value[:1], value[1:] + more]
            rs_send("two", part, way, jnp.concatenate(parts, axis=0), 2 * sign)

    def rsend(part):
        value = q[pl.ds(2 * halves[part], 2), z]
        for way in (0, 1):
            value = value + rs_got("one", part, way) + rs_got("two", part, way)
        q[pl.ds(2 * halves[part], 2), z] = value

    def rsline():
        sent["line"] = []
        for k in (1, 2, 3):
            line_out[k - 1] = q[flip(yl, k), z].astype(BF16)
            sent["line"].append(copy(line_out.at[k - 1], line_in.at[k - 1], near_y[k - 1]))

    def igrad():
        arrived(*sent["line"])
        igrad_ref[...] = (
            q[yl, z] + line_in[0].astype(F32) + line_in[1].astype(F32) + line_in[2].astype(F32)
        ).astype(BF16)

    f_halves = (1 - yh, yh)

    def fwd(part):
        gathers["f"].finish()
        loaded(0, 3)
        j = f_halves[part]
        rows = xf[pl.ds(2 * j, 2)].reshape(256, 768)

        def body(n, carry):
            at = pl.ds(pl.multiple_of(n * TILE, TILE), TILE)
            value = jnp.dot(rows, w[:, at], preferred_element_type=F32).reshape(4, 2, 32, TILE)
            p[part, :, :, :, at] = value
            x_out[part, :, :, :, at] = value.astype(BF16)
            return carry

        lax.fori_loop(0, 3, body, 0)
        sent["x", part] = [
            copy(x_out.at[part, there, c], x_in.at[part, i], d)
            for i, ((there, c), d) in enumerate(zip(row_places, near_row))
        ]

    def fsum(part):
        arrived(*sent["x", part])
        value = p[part, x, core]
        for i in range(7):
            value = value + x_in[part, i].astype(F32)
        if part == 0:
            y_out[...] = value.astype(BF16)
            sent["y"] = copy(y_out, y_in, far_y)
        else:
            sums[...] = value

    def hid():
        loaded(5)
        arrived(sent["y"])
        hidden_ref[...] = gelu_tanh(sums[...] + y_in[...].astype(F32) + bias[...]).astype(BF16)

    def bg():
        bgrad_ref[...] = jnp.sum(g[...].reshape(512, 768).astype(F32), axis=0)

    def wg():
        gathers["b"].finish()
        loaded(4)

        def body(n, carry):
            at = pl.ds(pl.multiple_of(n * TILE, TILE), TILE)
            wgrad_ref[at, :] = lax.dot_general(
                xb[:, :, :, :, :, at].reshape(512, TILE), g[...].reshape(512, 768), (((0,), (0,)), ((), ())),
                preferred_element_type=F32,
            )
            return carry

        lax.fori_loop(0, 3, body, 0)

    single = dict(
        far=far, spread=spread, back=back, rs=rs, rsend=rsend, rsline=rsline, igrad=igrad,
        fwd=fwd, fsum=fsum, hid=hid, bg=bg, wg=wg,
    )
    for what, *at in ORDER:
        if what in gathers:
            if at == ["line"]:
                gathers[what].line()
            else:
                gathers[what].step(*at)
        else:
            single[what](*at)
    for c in started:
        c.wait_send()


def local(tokens_fwd, tokens_bwd, weight, bias, preact, upstream):
    hbm = pl.BlockSpec(memory_space=pltpu.HBM)
    vmem = pl.BlockSpec(memory_space=pltpu.VMEM)
    shapes = (
        jax.ShapeDtypeStruct((32, 768), BF16),
        jax.ShapeDtypeStruct((16, 768), BF16),
        jax.ShapeDtypeStruct((768, 768), F32),
        jax.ShapeDtypeStruct((768,), F32),
    )
    tokens_fwd, tokens_bwd, weight, bias, preact, upstream = [
        pltpu.with_memory_space_constraint(a, pltpu.HBM)
        for a in (tokens_fwd, tokens_bwd, weight, bias, preact, upstream)
    ]
    return pl.pallas_call(
        kernel,
        out_shape=shapes,
        in_specs=[hbm] * 6,
        out_specs=[vmem] * 4,
        scratch_shapes=[
            pltpu.VMEM((4, 2, 2, 2, 16, 768), BF16),
            pltpu.VMEM((4, 2, 2, 2, 16, 768), BF16),
            pltpu.VMEM((2, 4, 2, 32, 768), BF16),
            pltpu.VMEM((4, 8, 16, 768), F32),
            pltpu.VMEM((768, 768), BF16),
            pltpu.VMEM((768,), F32),
            pltpu.VMEM((32, 768), BF16),
            pltpu.VMEM((32, 768), BF16),
            pltpu.VMEM((2, 4, 2, 32, 768), F32),
            pltpu.VMEM((2, 4, 2, 32, 768), BF16),
            pltpu.VMEM((2, 7, 32, 768), BF16),
            pltpu.VMEM((32, 768), BF16),
            pltpu.VMEM((32, 768), BF16),
            pltpu.VMEM((28, 16, 768), BF16),
            pltpu.VMEM((28, 16, 768), BF16),
            pltpu.VMEM((3, 16, 768), BF16),
            pltpu.VMEM((3, 16, 768), BF16),
            pltpu.VMEM((32, 768), F32),
            pltpu.SemaphoreType.DMA((N_LOCAL,)),
            pltpu.SemaphoreType.DMA((N_REMOTE,)),
            pltpu.SemaphoreType.DMA((N_REMOTE,)),
        ],
        compiler_params=pltpu.CompilerParams(
            collective_id=0, has_side_effects=True, vmem_limit_bytes=48 * 2**20
        ),
        cost_estimate=pl.CostEstimate(flops=3 * 2 * 512 * 768 * 768, bytes_accessed=8 * 2**20, transcendentals=50000),
        name="feed_forward",
    )(tokens_fwd, tokens_bwd, weight, bias, preact, upstream)

def solution(mesh):
    return jax.shard_map(
        local,
        mesh=mesh,
        in_specs=(
            P("col", "row"),
            P("col", "row"),
            P("row", "col"),
            P("col"),
            P("row", "col"),
            P("row", "col"),
        ),
        out_specs=(P("row", "col"), P("col", "row"), P("row", "col"), P("col")),
        check_vma=False,
    )
```

```python
import math

import jax
import jax.numpy as jnp
from jax import lax
from jax.experimental import pallas as pl
from jax.experimental.pallas import tpu as pltpu
from jax.sharding import PartitionSpec as P

gelu_scale = math.sqrt(2.0 / math.pi)
cubic_term = 0.044715
F32, BF16 = jnp.float32, jnp.bfloat16
MESH = pl.DeviceIdType.MESH
TILE = 256


def gelu_tanh(values):
    inner_arg = gelu_scale * (values + cubic_term * values * values * values)
    return 0.5 * values * (1.0 + jnp.tanh(inner_arg))


def gelu_slope(values):
    tangent = jnp.tanh(gelu_scale * (values + cubic_term * values * values * values))
    return 0.5 * (1.0 + tangent) + 0.5 * values * (1.0 - tangent * tangent) * gelu_scale * (
        1.0 + 3.0 * cubic_term * values * values
    )


def flip(i, k):
    if k == 1:
        return i + 1 - 2 * lax.rem(i, 2)
    if k == 2:
        return lax.rem(i + 2, 4)
    return 3 - i


class Copies:
    def __init__(self, extent, send, recv):
        self.extent, self.send, self.recv = extent, send, recv
        self.groups, self.waited, self.sent = {}, set(), 0

    def start(self, src, dst, target, group):
        rows = math.prod(dst.shape) // 768
        number, before = self.groups.get(group, (len(self.groups), 0))
        self.groups[group] = (number, before + rows)
        self.sent += rows
        pltpu.make_async_remote_copy(
            src_ref=src, dst_ref=dst, send_sem=self.send, recv_sem=self.recv.at[number],
            device_id=target, device_id_type=MESH,
        ).start()

    def whole(self, rows, number, target):
        extent = self.extent.at[pl.ds(0, rows)]
        return pltpu.make_async_remote_copy(
            src_ref=extent, dst_ref=extent, send_sem=self.send, recv_sem=self.recv.at[number],
            device_id=target, device_id_type=MESH,
        )

    def arrived(self, target, *groups):
        for group in groups:
            if group not in self.waited:
                self.waited.add(group)
                number, rows = self.groups[group]
                self.whole(rows, number, target).wait_recv()

    def finish(self, target):
        self.whole(self.sent, 0, target).wait_send()


ORDER = (
    ("b", 0, 0, 0), ("f", "line"), ("f", 0, 0, 0), ("far",), ("f", 0, 1, 0), ("spread", 0), ("b", 1, 0, 0),
    ("b", 1, 0, 1), ("f", 0, 2, 0), ("f", 1, 1, 1), ("f", 1, 0, 1), ("spread", 1), ("b", "line"), ("f", 1, 1, 0),
    ("f", 1, 0, 0), ("f", 1, 2, 1), ("f", 1, 2, 0), ("back", 0), ("rs", 0, 0, 1), ("rs", 0, 0, 0), ("back", 1),
    ("rs", 0, 1, 0), ("rs", 0, 1, 1), ("fwd", 0), ("rs", 1, 0, 1), ("rs", 1, 0, 0), ("rs", 1, 1, 0), ("rs", 1, 1, 1),
    ("fwd", 1), ("fsum", 0), ("rsend", 0), ("rsend", 1), ("rsline",), ("wg",), ("fsum", 1), ("bg",), ("hid",),
    ("igrad",),
)


RS_SLOT = {"three": 0, "four": 2, "one": 3, "two": 5}
RS_SIZE = {"three": 2, "four": 1, "one": 2, "two": 2}
N_LOCAL = 6
N_GROUPS = 26
SENT_ROWS = 2448


def kernel(
    fwd_hbm, bwd_hbm, w_hbm, bias_hbm, pre_hbm, up_hbm,
    hidden_ref, igrad_ref, wgrad_ref, bgrad_ref,
    xf, xb, g, q, w, bias, pre, up,
    p, x_out, x_in, y_out, y_in,
    rs_out, rs_in, line_out, line_in, sums,
    extent, local_sem, send_sem, recv_sem,
):
    row, col = lax.axis_index("row"), lax.axis_index("col")
    yh, x, core = row // 8, lax.rem(row // 2, 4), lax.rem(row, 2)
    yl, z = col // 8, lax.rem(col, 8)
    mate, opposite = flip(yl, 1), 1 - yl // 2

    def device(yh=yh, x=x, core=core, yl=yl, z=z):
        return (yh * 8 + x * 2 + core, yl * 8 + z)

    along_z = {away: device(z=lax.rem(z + away + 8, 8)) for away in (1, -1, 2, -2)}
    near_z = (along_z[1], along_z[-1])
    near_y = [device(yl=flip(yl, k)) for k in (1, 2, 3)]
    far_y = device(yh=1 - yh)
    row_places = [(flip(x, k) if k else x, c) for k, c in ((2, 1 - core), (2, core), (1, 1 - core), (3, 1 - core), (1, core), (3, core), (0, 1 - core))]
    near_row = [device(x=there, core=c) for there, c in row_places]
    partners = [*along_z.values(), *near_y, far_y, *near_row]

    copies = Copies(extent, send_sem, recv_sem)
    copy = copies.start

    def arrived(*groups):
        copies.arrived(near_z[0], *groups)

    def at_z(at):
        return at // 4, lax.rem(at // 2, 2), lax.rem(at, 2)

    loads = [
        pltpu.make_async_copy(src, dst, local_sem.at[i])
        for i, (src, dst) in enumerate(
            [
                (fwd_hbm, xf.at[(yl, *at_z(z))]), (pre_hbm, pre), (up_hbm, up), (w_hbm, w),
                (bwd_hbm, xb.at[(yl, *at_z(z))]), (bias_hbm, bias),
            ]
        )
    ]
    barrier = pltpu.get_barrier_semaphore()
    for d in partners:
        pl.semaphore_signal(barrier, inc=1, device_id=d, device_id_type=MESH)
    for c in loads:
        c.start()
    loads[1].wait()
    loads[2].wait()
    g[yh, x, core] = (up[...].astype(F32) * gelu_slope(pre[...].astype(F32))).astype(BF16)
    pl.semaphore_wait(barrier, len(partners))

    waited = {1, 2}

    def loaded(*which):
        for i in which:
            if i not in waited:
                waited.add(i)
                loads[i].wait()

    class Gather:
        def __init__(self, name, hbm, ref, z_first):
            self.name, self.hbm, self.ref, self.z_first = name, hbm, ref, z_first

        def line(self):
            if self.z_first:
                arrived((self.name, "rest"))
                loaded(4)
                block = src = self.ref.at[yl]
            else:
                block, src = self.ref.at[(yl, *at_z(z))], self.hbm
            for k in (1, 2, 3):
                copy(src, block, near_y[k - 1], (self.name, "line", 0 if self.z_first else min(k, 2)))

        def block(self, which, source):
            if which == 0:
                return self.ref.at[(yl, *at_z(source))]
            rows = pl.ds(mate, 1) if which == 1 else pl.ds(2 * opposite, 2)
            return self.ref.at[(rows, *at_z(source))]

        def step(self, s, which, way):
            if s == 0:
                if which:
                    arrived((self.name, "line", which))
                block = self.block(which, z)
                src = block if which else self.hbm
                for way in (0, 1):
                    copy(src, block, along_z[(2, -2)[way]], (self.name, 2, which, way))
                for way in (0, 1):
                    copy(src, block, along_z[(1, -1)[way]], (self.name, "rest"))
                return
            arrived((self.name, 2, which, way))
            sign = (1, -1)[way]
            source = lax.rem(z - 2 * sign + 8, 8)
            if which == 2 or which == way:
                half = self.ref.at[(2 * opposite + way, *at_z(source))] if which == 2 else self.block(which, source)
                copy(half, half, along_z[2 * sign], (self.name, "rest"))
            block = self.block(which, source)
            copy(block, block, along_z[sign], (self.name, "rest"))

        def finish(self):
            arrived((self.name, "line", 0) if self.z_first else (self.name, "rest"))

    gathers = {"f": Gather("f", fwd_hbm, xf, False), "b": Gather("b", bwd_hbm, xb, True)}

    def far():
        copy(g.at[yh, x, core], g.at[yh, x, core], far_y, "far")

    def spread(half):
        if half == 1:
            arrived("far")
        at = (yh, 1 - yh)[half]
        for d in near_row:
            copy(g.at[at, x, core], g.at[at, x, core], d, ("spread", half))

    halves = (yh, 1 - yh)

    def back(part):
        arrived(("spread", part))
        loaded(3)
        j = halves[part]
        rows = g[j].reshape(256, 768)

        def body(n, carry):
            at = pl.ds(pl.multiple_of(n * TILE, TILE), TILE)
            q[pl.ds(2 * j, 2), :, :, at] = lax.dot_general(
                rows, w[at, :], (((1,), (1,)), ((), ())), preferred_element_type=F32
            ).reshape(2, 8, 16, TILE)
            return carry

        lax.fori_loop(0, 3, body, 0)

    def rs_send(name, part, way, value, away, group):
        slots = pl.ds(RS_SLOT[name] + 7 * (2 * part + way), value.shape[0])
        rs_out[slots] = value.astype(BF16)
        copy(rs_out.at[slots], rs_in.at[slots], along_z[away], group)

    def rs_got(name, part, way):
        return rs_in[pl.ds(RS_SLOT[name] + 7 * (2 * part + way), RS_SIZE[name])].astype(F32)

    def rs(s, part, way):
        j, sign = halves[part], (1, -1)[way]

        def sums_for(away):
            return q[pl.ds(2 * j, 2), lax.rem(z + sign * away + 8, 8)]

        if s == 0:
            rs_send("three", part, way, sums_for(3), sign, ("mid", part, way))
            rs_send("four", part, way, q[pl.ds(2 * j + way, 1), lax.rem(z + 4, 8)], 2 * sign, ("mid", part, way))
            rs_send("one", part, way, sums_for(1), sign, ("end", part))
        else:
            arrived(("mid", part, way))
            value = sums_for(2) + rs_got("three", part, way)
            more = rs_got("four", part, way)
            parts = [value[:1] + more, value[1:]] if way == 0 else [value[:1], value[1:] + more]
            rs_send("two", part, way, jnp.concatenate(parts, axis=0), 2 * sign, ("end", part))

    def rsend(part):
        arrived(("end", part))
        value = q[pl.ds(2 * halves[part], 2), z]
        for way in (0, 1):
            value = value + rs_got("one", part, way) + rs_got("two", part, way)
        q[pl.ds(2 * halves[part], 2), z] = value

    def rsline():
        for k in (1, 2, 3):
            line_out[k - 1] = q[flip(yl, k), z].astype(BF16)
            copy(line_out.at[k - 1], line_in.at[k - 1], near_y[k - 1], "line")

    def igrad():
        arrived("line")
        igrad_ref[...] = (
            q[yl, z] + line_in[0].astype(F32) + line_in[1].astype(F32) + line_in[2].astype(F32)
        ).astype(BF16)

    f_halves = (1 - yh, yh)

    def fwd(part):
        gathers["f"].finish()
        loaded(0, 3)
        j = f_halves[part]
        rows = xf[pl.ds(2 * j, 2)].reshape(256, 768)

        def body(n, carry):
            at = pl.ds(pl.multiple_of(n * TILE, TILE), TILE)
            value = jnp.dot(rows, w[:, at], preferred_element_type=F32).reshape(4, 2, 32, TILE)
            p[part, :, :, :, at] = value
            x_out[part, :, :, :, at] = value.astype(BF16)
            return carry

        lax.fori_loop(0, 3, body, 0)
        for i, ((there, c), d) in enumerate(zip(row_places, near_row)):
            copy(x_out.at[part, there, c], x_in.at[part, i], d, ("x", part))

    def fsum(part):
        arrived(("x", part))
        value = p[part, x, core]
        for i in range(7):
            value = value + x_in[part, i].astype(F32)
        if part == 0:
            y_out[...] = value.astype(BF16)
            copy(y_out, y_in, far_y, "y")
        else:
            sums[...] = value

    def hid():
        loaded(5)
        arrived("y")
        hidden_ref[...] = gelu_tanh(sums[...] + y_in[...].astype(F32) + bias[...]).astype(BF16)

    def bg():
        bgrad_ref[...] = jnp.sum(g[...].reshape(512, 768).astype(F32), axis=0)

    def wg():
        gathers["b"].finish()
        loaded(4)

        def body(n, carry):
            at = pl.ds(pl.multiple_of(n * TILE, TILE), TILE)
            wgrad_ref[at, :] = lax.dot_general(
                xb[:, :, :, :, :, at].reshape(512, TILE), g[...].reshape(512, 768), (((0,), (0,)), ((), ())),
                preferred_element_type=F32,
            )
            return carry

        lax.fori_loop(0, 3, body, 0)

    single = dict(
        far=far, spread=spread, back=back, rs=rs, rsend=rsend, rsline=rsline, igrad=igrad,
        fwd=fwd, fsum=fsum, hid=hid, bg=bg, wg=wg,
    )
    for what, *at in ORDER:
        if what in gathers:
            if at == ["line"]:
                gathers[what].line()
            else:
                gathers[what].step(*at)
        else:
            single[what](*at)
    copies.finish(near_z[0])


def local(tokens_fwd, tokens_bwd, weight, bias, preact, upstream):
    hbm = pl.BlockSpec(memory_space=pltpu.HBM)
    vmem = pl.BlockSpec(memory_space=pltpu.VMEM)
    shapes = (
        jax.ShapeDtypeStruct((32, 768), BF16),
        jax.ShapeDtypeStruct((16, 768), BF16),
        jax.ShapeDtypeStruct((768, 768), F32),
        jax.ShapeDtypeStruct((768,), F32),
    )
    tokens_fwd, tokens_bwd, weight, bias, preact, upstream = [
        pltpu.with_memory_space_constraint(a, pltpu.HBM)
        for a in (tokens_fwd, tokens_bwd, weight, bias, preact, upstream)
    ]
    return pl.pallas_call(
        kernel,
        out_shape=shapes,
        in_specs=[hbm] * 6,
        out_specs=[vmem] * 4,
        scratch_shapes=[
            pltpu.VMEM((4, 2, 2, 2, 16, 768), BF16),
            pltpu.VMEM((4, 2, 2, 2, 16, 768), BF16),
            pltpu.VMEM((2, 4, 2, 32, 768), BF16),
            pltpu.VMEM((4, 8, 16, 768), F32),
            pltpu.VMEM((768, 768), BF16),
            pltpu.VMEM((768,), F32),
            pltpu.VMEM((32, 768), BF16),
            pltpu.VMEM((32, 768), BF16),
            pltpu.VMEM((2, 4, 2, 32, 768), F32),
            pltpu.VMEM((2, 4, 2, 32, 768), BF16),
            pltpu.VMEM((2, 7, 32, 768), BF16),
            pltpu.VMEM((32, 768), BF16),
            pltpu.VMEM((32, 768), BF16),
            pltpu.VMEM((28, 16, 768), BF16),
            pltpu.VMEM((28, 16, 768), BF16),
            pltpu.VMEM((3, 16, 768), BF16),
            pltpu.VMEM((3, 16, 768), BF16),
            pltpu.VMEM((32, 768), F32),
            pltpu.VMEM((SENT_ROWS, 768), BF16),
            pltpu.SemaphoreType.DMA((N_LOCAL,)),
            pltpu.SemaphoreType.DMA,
            pltpu.SemaphoreType.DMA((N_GROUPS,)),
        ],
        compiler_params=pltpu.CompilerParams(
            collective_id=0, has_side_effects=True, vmem_limit_bytes=48 * 2**20
        ),
        cost_estimate=pl.CostEstimate(flops=3 * 2 * 512 * 768 * 768, bytes_accessed=8 * 2**20, transcendentals=50000),
        name="feed_forward",
    )(tokens_fwd, tokens_bwd, weight, bias, preact, upstream)

def solution(mesh):
    return jax.shard_map(
        local,
        mesh=mesh,
        in_specs=(
            P("col", "row"),
            P("col", "row"),
            P("row", "col"),
            P("col"),
            P("row", "col"),
            P("row", "col"),
        ),
        out_specs=(P("row", "col"), P("col", "row"), P("row", "col"), P("col")),
        check_vma=False,
    )
```

```python
import math

import jax
import jax.numpy as jnp
from jax import lax
from jax.experimental import pallas as pl
from jax.experimental.pallas import tpu as pltpu
from jax.sharding import PartitionSpec as P

gelu_scale = math.sqrt(2.0 / math.pi)
cubic_term = 0.044715
F32, BF16 = jnp.float32, jnp.bfloat16
MESH = pl.DeviceIdType.MESH
TILE = 256


def gelu_tanh(values):
    inner_arg = gelu_scale * (values + cubic_term * values * values * values)
    return 0.5 * values * (1.0 + jnp.tanh(inner_arg))


def gelu_slope(values):
    tangent = jnp.tanh(gelu_scale * (values + cubic_term * values * values * values))
    return 0.5 * (1.0 + tangent) + 0.5 * values * (1.0 - tangent * tangent) * gelu_scale * (
        1.0 + 3.0 * cubic_term * values * values
    )


def flip(i, k):
    if k == 1:
        return i + 1 - 2 * lax.rem(i, 2)
    if k == 2:
        return lax.rem(i + 2, 4)
    return 3 - i


class Copies:
    def __init__(self, extent, send, recv):
        self.extent, self.send, self.recv = extent, send, recv
        self.groups, self.waited, self.sent = {}, set(), 0

    def start(self, src, dst, target, group):
        rows = math.prod(dst.shape) // 768
        number, before = self.groups.get(group, (len(self.groups), 0))
        self.groups[group] = (number, before + rows)
        self.sent += rows
        pltpu.make_async_remote_copy(
            src_ref=src, dst_ref=dst, send_sem=self.send, recv_sem=self.recv.at[number],
            device_id=target, device_id_type=MESH,
        ).start()

    def whole(self, rows, number, target):
        extent = self.extent.at[pl.ds(0, rows)]
        return pltpu.make_async_remote_copy(
            src_ref=extent, dst_ref=extent, send_sem=self.send, recv_sem=self.recv.at[number],
            device_id=target, device_id_type=MESH,
        )

    def arrived(self, target, *groups):
        for group in groups:
            if group not in self.waited:
                self.waited.add(group)
                number, rows = self.groups[group]
                self.whole(rows, number, target).wait_recv()

    def finish(self, target):
        self.whole(self.sent, 0, target).wait_send()


ORDER = (
    ("b", 0, 0, 0), ("f", "line"), ("f", 0, 0, 0), ("far",), ("f", 0, 1, 0), ("spread", 0), ("b", 1, 0, 0),
    ("b", 1, 0, 1), ("f", 0, 2, 0), ("f", 1, 1, 1), ("f", 1, 0, 1), ("spread", 1), ("b", "line"), ("f", 1, 1, 0),
    ("f", 1, 0, 0), ("f", 1, 2, 1), ("f", 1, 2, 0), ("back", 0), ("rs", 0, 0, 1), ("rs", 0, 0, 0), ("back", 1),
    ("rs", 0, 1, 0), ("rs", 0, 1, 1), ("fwd", 0), ("rs", 1, 0, 1), ("rs", 1, 0, 0), ("rs", 1, 1, 0), ("rs", 1, 1, 1),
    ("fwd", 1), ("fsum", 0), ("rsend", 0), ("rsend", 1), ("rsline",), ("wg",), ("fsum", 1), ("bg",), ("hid",),
    ("igrad",),
)


RS_SLOT = {"three": 0, "four": 2, "one": 3, "two": 5}
RS_SIZE = {"three": 2, "four": 1, "one": 2, "two": 2}
N_LOCAL = 6
N_GROUPS = 26
SENT_ROWS = 2448


def kernel(
    fwd_hbm, bwd_hbm, w_hbm, bias_hbm, pre_hbm, up_hbm,
    hidden_ref, igrad_ref, wgrad_ref, bgrad_ref,
    xf, xb, g, q, w, bias, pre, up,
    p, x_out, x_in, y_out, y_in,
    rs_out, rs_in, line_out, line_in, sums,
    extent, local_sem, send_sem, recv_sem,
):
    row, col = lax.axis_index("row"), lax.axis_index("col")
    yh, x, core = row // 8, lax.rem(row // 2, 4), lax.rem(row, 2)
    yl, z = col // 8, lax.rem(col, 8)
    mate, opposite = flip(yl, 1), 1 - yl // 2

    def device(yh=yh, x=x, core=core, yl=yl, z=z):
        return (yh * 8 + x * 2 + core, yl * 8 + z)

    along_z = {away: device(z=lax.rem(z + away + 8, 8)) for away in (1, -1, 2, -2)}
    near_z = (along_z[1], along_z[-1])
    near_y = [device(yl=flip(yl, k)) for k in (1, 2, 3)]
    far_y = device(yh=1 - yh)
    row_places = [(flip(x, k) if k else x, c) for k, c in ((2, 1 - core), (2, core), (1, 1 - core), (3, 1 - core), (1, core), (3, core), (0, 1 - core))]
    near_row = [device(x=there, core=c) for there, c in row_places]
    partners = [*along_z.values(), *near_y, far_y, *near_row]

    copies = Copies(extent, send_sem, recv_sem)
    copy = copies.start

    def arrived(*groups):
        copies.arrived(near_z[0], *groups)

    def at_z(at):
        return at // 4, lax.rem(at // 2, 2), lax.rem(at, 2)

    loads = [
        pltpu.make_async_copy(src, dst, local_sem.at[i])
        for i, (src, dst) in enumerate(
            [
                (fwd_hbm, xf.at[(yl, *at_z(z))]), (pre_hbm, pre), (up_hbm, up), (w_hbm, w),
                (bwd_hbm, xb.at[(yl, *at_z(z))]), (bias_hbm, bias),
            ]
        )
    ]
    barrier = pltpu.get_barrier_semaphore()
    for d in partners:
        pl.semaphore_signal(barrier, inc=1, device_id=d, device_id_type=MESH)
    for c in loads:
        c.start()
    loads[1].wait()
    loads[2].wait()
    g[yh, x, core] = (up[...].astype(F32) * gelu_slope(pre[...].astype(F32))).astype(BF16)
    pl.semaphore_wait(barrier, len(partners))

    waited = {1, 2}

    def loaded(*which):
        for i in which:
            if i not in waited:
                waited.add(i)
                loads[i].wait()

    class Gather:
        def __init__(self, name, hbm, ref, z_first):
            self.name, self.hbm, self.ref, self.z_first = name, hbm, ref, z_first

        def line(self):
            if self.z_first:
                arrived((self.name, "rest"))
                loaded(4)
                block = src = self.ref.at[yl]
            else:
                block, src = self.ref.at[(yl, *at_z(z))], self.hbm
            for k in (1, 2, 3):
                copy(src, block, near_y[k - 1], (self.name, "line", 0 if self.z_first else min(k, 2)))

        def block(self, which, source):
            if which == 0:
                return self.ref.at[(yl, *at_z(source))]
            rows = pl.ds(mate, 1) if which == 1 else pl.ds(2 * opposite, 2)
            return self.ref.at[(rows, *at_z(source))]

        def step(self, s, which, way):
            if s == 0:
                if which:
                    arrived((self.name, "line", which))
                block = self.block(which, z)
                src = block if which else self.hbm
                for way in (0, 1):
                    copy(src, block, along_z[(2, -2)[way]], (self.name, 2, which, way))
                for way in (0, 1):
                    copy(src, block, along_z[(1, -1)[way]], (self.name, "rest"))
                return
            arrived((self.name, 2, which, way))
            sign = (1, -1)[way]
            source = lax.rem(z - 2 * sign + 8, 8)
            if which == 2 or which == way:
                half = self.ref.at[(2 * opposite + way, *at_z(source))] if which == 2 else self.block(which, source)
                copy(half, half, along_z[2 * sign], (self.name, "rest"))
            block = self.block(which, source)
            copy(block, block, along_z[sign], (self.name, "rest"))

        def finish(self):
            arrived((self.name, "line", 0) if self.z_first else (self.name, "rest"))

    gathers = {"f": Gather("f", fwd_hbm, xf, False), "b": Gather("b", bwd_hbm, xb, True)}

    def far():
        copy(g.at[yh, x, core], g.at[yh, x, core], far_y, "far")

    def spread(half):
        if half == 1:
            arrived("far")
        at = (yh, 1 - yh)[half]
        for d in near_row:
            copy(g.at[at, x, core], g.at[at, x, core], d, ("spread", half))

    halves = (yh, 1 - yh)

    def back(part):
        arrived(("spread", part))
        loaded(3)
        j = halves[part]
        rows = g[j].reshape(256, 768)

        def body(n, carry):
            at = pl.ds(pl.multiple_of(n * TILE, TILE), TILE)
            q[pl.ds(2 * j, 2), :, :, at] = lax.dot_general(
                rows, w[at, :], (((1,), (1,)), ((), ())), preferred_element_type=F32
            ).reshape(2, 8, 16, TILE)
            return carry

        lax.fori_loop(0, 3, body, 0)

    def rs_send(name, part, way, value, away, group):
        slots = pl.ds(RS_SLOT[name] + 7 * (2 * part + way), value.shape[0])
        rs_out[slots] = value.astype(BF16)
        copy(rs_out.at[slots], rs_in.at[slots], along_z[away], group)

    def rs_got(name, part, way):
        return rs_in[pl.ds(RS_SLOT[name] + 7 * (2 * part + way), RS_SIZE[name])].astype(F32)

    def rs(s, part, way):
        j, sign = halves[part], (1, -1)[way]

        def sums_for(away):
            return q[pl.ds(2 * j, 2), lax.rem(z + sign * away + 8, 8)]

        if s == 0:
            rs_send("three", part, way, sums_for(3), sign, ("mid", part, way))
            rs_send("four", part, way, q[pl.ds(2 * j + way, 1), lax.rem(z + 4, 8)], 2 * sign, ("mid", part, way))
            rs_send("one", part, way, sums_for(1), sign, ("end", part))
        else:
            arrived(("mid", part, way))
            value = sums_for(2) + rs_got("three", part, way)
            more = rs_got("four", part, way)
            parts = [value[:1] + more, value[1:]] if way == 0 else [value[:1], value[1:] + more]
            rs_send("two", part, way, jnp.concatenate(parts, axis=0), 2 * sign, ("end", part))

    def rsend(part):
        arrived(("end", part))
        value = q[pl.ds(2 * halves[part], 2), z]
        for way in (0, 1):
            value = value + rs_got("one", part, way) + rs_got("two", part, way)
        q[pl.ds(2 * halves[part], 2), z] = value

    def rsline():
        for k in (1, 2, 3):
            line_out[k - 1] = q[flip(yl, k), z].astype(BF16)
            copy(line_out.at[k - 1], line_in.at[k - 1], near_y[k - 1], "line")

    def igrad():
        arrived("line")
        igrad_ref[...] = (
            q[yl, z] + line_in[0].astype(F32) + line_in[1].astype(F32) + line_in[2].astype(F32)
        ).astype(BF16)

    f_halves = (1 - yh, yh)

    def fwd(part):
        gathers["f"].finish()
        loaded(0, 3)
        j = f_halves[part]
        rows = xf[pl.ds(2 * j, 2)].reshape(256, 768)

        def body(n, carry):
            at = pl.ds(pl.multiple_of(n * TILE, TILE), TILE)
            value = jnp.dot(rows, w[:, at], preferred_element_type=F32).reshape(4, 2, 32, TILE)
            p[part, :, :, :, at] = value
            x_out[part, :, :, :, at] = value.astype(BF16)
            return carry

        lax.fori_loop(0, 3, body, 0)
        for i, ((there, c), d) in enumerate(zip(row_places, near_row)):
            copy(x_out.at[part, there, c], x_in.at[part, i], d, ("x", part))

    def fsum(part):
        arrived(("x", part))
        value = p[part, x, core]
        for i in range(7):
            value = value + x_in[part, i].astype(F32)
        if part == 0:
            y_out[...] = value.astype(BF16)
            copy(y_out, y_in, far_y, "y")
        else:
            sums[...] = value

    def hid():
        loaded(5)
        arrived("y")
        hidden_ref[...] = gelu_tanh(sums[...] + y_in[...].astype(F32) + bias[...]).astype(BF16)

    def bg():
        bgrad_ref[...] = jnp.sum(g[...].reshape(512, 768).astype(F32), axis=0)

    def wg():
        gathers["b"].finish()
        loaded(4)

        def body(n, carry):
            at = pl.ds(pl.multiple_of(n * TILE, TILE), TILE)
            wgrad_ref[at, :] = lax.dot_general(
                xb[:, :, :, :, :, at].reshape(512, TILE), g[...].reshape(512, 768), (((0,), (0,)), ((), ())),
                preferred_element_type=F32,
            )
            return carry

        lax.fori_loop(0, 3, body, 0)

    single = dict(
        far=far, spread=spread, back=back, rs=rs, rsend=rsend, rsline=rsline, igrad=igrad,
        fwd=fwd, fsum=fsum, hid=hid, bg=bg, wg=wg,
    )
    for what, *at in ORDER:
        if what in gathers:
            if at == ["line"]:
                gathers[what].line()
            else:
                gathers[what].step(*at)
        else:
            single[what](*at)
    copies.finish(near_z[0])


def finish(*refs):
    sem = refs[-1]
    moves = [pltpu.make_async_copy(refs[i], refs[4 + i], sem.at[i]) for i in range(4)]
    for c in moves:
        c.start()
    for c in moves:
        c.wait()


def local(tokens_fwd, tokens_bwd, weight, bias, preact, upstream):
    hbm = pl.BlockSpec(memory_space=pltpu.HBM)
    vmem = pl.BlockSpec(memory_space=pltpu.VMEM)
    shapes = (
        jax.ShapeDtypeStruct((32, 768), BF16),
        jax.ShapeDtypeStruct((16, 768), BF16),
        jax.ShapeDtypeStruct((768, 768), F32),
        jax.ShapeDtypeStruct((768,), F32),
    )
    tokens_fwd, tokens_bwd, weight, bias, preact, upstream = [
        pltpu.with_memory_space_constraint(a, pltpu.HBM)
        for a in (tokens_fwd, tokens_bwd, weight, bias, preact, upstream)
    ]
    results = pl.pallas_call(
        kernel,
        out_shape=shapes,
        in_specs=[hbm] * 6,
        out_specs=[vmem] * 4,
        scratch_shapes=[
            pltpu.VMEM((4, 2, 2, 2, 16, 768), BF16),
            pltpu.VMEM((4, 2, 2, 2, 16, 768), BF16),
            pltpu.VMEM((2, 4, 2, 32, 768), BF16),
            pltpu.VMEM((4, 8, 16, 768), F32),
            pltpu.VMEM((768, 768), BF16),
            pltpu.VMEM((768,), F32),
            pltpu.VMEM((32, 768), BF16),
            pltpu.VMEM((32, 768), BF16),
            pltpu.VMEM((2, 4, 2, 32, 768), F32),
            pltpu.VMEM((2, 4, 2, 32, 768), BF16),
            pltpu.VMEM((2, 7, 32, 768), BF16),
            pltpu.VMEM((32, 768), BF16),
            pltpu.VMEM((32, 768), BF16),
            pltpu.VMEM((28, 16, 768), BF16),
            pltpu.VMEM((28, 16, 768), BF16),
            pltpu.VMEM((3, 16, 768), BF16),
            pltpu.VMEM((3, 16, 768), BF16),
            pltpu.VMEM((32, 768), F32),
            pltpu.VMEM((SENT_ROWS, 768), BF16),
            pltpu.SemaphoreType.DMA((N_LOCAL,)),
            pltpu.SemaphoreType.DMA,
            pltpu.SemaphoreType.DMA((N_GROUPS,)),
        ],
        compiler_params=pltpu.CompilerParams(
            collective_id=0, has_side_effects=True, vmem_limit_bytes=48 * 2**20
        ),
        cost_estimate=pl.CostEstimate(flops=3 * 2 * 512 * 768 * 768, bytes_accessed=8 * 2**20, transcendentals=50000),
        name="feed_forward",
    )(tokens_fwd, tokens_bwd, weight, bias, preact, upstream)
    return pl.pallas_call(
        finish,
        out_shape=tuple(jax.ShapeDtypeStruct(r.shape, r.dtype) for r in results),
        in_specs=[pl.BlockSpec(memory_space=pltpu.VMEM)] * 4,
        out_specs=[pl.BlockSpec(memory_space=pl.ANY)] * 4,
        scratch_shapes=[pltpu.SemaphoreType.DMA((4,))],
        compiler_params=pltpu.CompilerParams(vmem_limit_bytes=1 << 20),
        name="write_out",
    )(*results)

def solution(mesh):
    return jax.shard_map(
        local,
        mesh=mesh,
        in_specs=(
            P("col", "row"),
            P("col", "row"),
            P("row", "col"),
            P("col"),
            P("row", "col"),
            P("row", "col"),
        ),
        out_specs=(P("row", "col"), P("col", "row"), P("row", "col"), P("col")),
        check_vma=False,
    )
```

```python
import math

import jax
import jax.numpy as jnp
from jax import lax
from jax.experimental import pallas as pl
from jax.experimental.pallas import tpu as pltpu
from jax.sharding import PartitionSpec as P

gelu_scale = math.sqrt(2.0 / math.pi)
cubic_term = 0.044715
F32, BF16 = jnp.float32, jnp.bfloat16
MESH = pl.DeviceIdType.MESH
TILE = 384


def gelu_tanh(values):
    inner_arg = gelu_scale * (values + cubic_term * values * values * values)
    return 0.5 * values * (1.0 + jnp.tanh(inner_arg))


def gelu_slope(values):
    tangent = jnp.tanh(gelu_scale * (values + cubic_term * values * values * values))
    return 0.5 * (1.0 + tangent) + 0.5 * values * (1.0 - tangent * tangent) * gelu_scale * (
        1.0 + 3.0 * cubic_term * values * values
    )


def flip(i, k):
    if k == 1:
        return i + 1 - 2 * lax.rem(i, 2)
    if k == 2:
        return lax.rem(i + 2, 4)
    return 3 - i


class Copies:
    def __init__(self, extent, send, recv):
        self.extent, self.send, self.recv = extent, send, recv
        self.groups, self.waited, self.sent = {}, set(), 0

    def start(self, src, dst, target, group, again=False):
        rows = 0 if again else math.prod(dst.shape) // 768
        number, before = self.groups.get(group, (len(self.groups), 0))
        self.groups[group] = (number, before + rows)
        self.sent += rows
        pltpu.make_async_remote_copy(
            src_ref=src, dst_ref=dst, send_sem=self.send, recv_sem=self.recv.at[number],
            device_id=target, device_id_type=MESH,
        ).start()

    def whole(self, rows, number, target):
        extent = self.extent.at[pl.ds(0, rows)]
        return pltpu.make_async_remote_copy(
            src_ref=extent, dst_ref=extent, send_sem=self.send, recv_sem=self.recv.at[number],
            device_id=target, device_id_type=MESH,
        )

    def arrived(self, target, *groups):
        for group in groups:
            if group not in self.waited:
                self.waited.add(group)
                number, rows = self.groups[group]
                self.whole(rows, number, target).wait_recv()

    def finish(self, target):
        self.whole(self.sent, 0, target).wait_send()


ORDER = (
    ("f", "line"), ("spread", 0), ("b", 0, 0, 0), ("f", 0, 0, 0), ("far",), ("f", 0, 1, 0), ("b", 1, 0, 0),
    ("b", 1, 0, 1), ("f", 0, 2, 0), ("spread", 1), ("back", 0), ("rs", 0, 0, 1), ("b", "line"), ("f", 1, 0, 0),
    ("f", 1, 2, 1), ("f", 1, 0, 1), ("f", 1, 1, 1), ("f", 1, 1, 0), ("f", 1, 2, 0), ("rs", 0, 0, 0), ("fwd", 0),
    ("back", 1), ("rs", 0, 1, 0), ("rs", 0, 1, 1), ("fwd", 1), ("rs", 1, 0, 1), ("rs", 1, 0, 0), ("rs", 1, 1, 0),
    ("rs", 1, 1, 1), ("fsum", 0), ("bg",), ("rsend", 0), ("rsend", 1), ("rsline",), ("wg",), ("fsum", 1), ("hid",),
    ("igrad",),
)


RS_SLOT = {"three": 0, "four": 2, "one": 3, "two": 5}
RS_SIZE = {"three": 2, "four": 1, "one": 2, "two": 2}
N_LOCAL = 6
N_GROUPS = 28
SENT_ROWS = 2448


def kernel(
    fwd_hbm, bwd_hbm, w_hbm, bias_hbm, pre_hbm, up_hbm,
    hidden_ref, igrad_ref, wgrad_ref, bgrad_ref,
    xf, xb, g, q, w, bias, pre, up,
    p, x_out, x_in, y_out, y_in,
    rs_out, rs_in, line_out, line_in, sums,
    extent, local_sem, send_sem, recv_sem,
):
    row, col = lax.axis_index("row"), lax.axis_index("col")
    yh, x, core = row // 8, lax.rem(row // 2, 4), lax.rem(row, 2)
    yl, z = col // 8, lax.rem(col, 8)
    mate, opposite = flip(yl, 1), 1 - yl // 2

    def device(yh=yh, x=x, core=core, yl=yl, z=z):
        return (yh * 8 + x * 2 + core, yl * 8 + z)

    along_z = {away: device(z=lax.rem(z + away + 8, 8)) for away in (1, -1, 2, -2)}
    near_z = (along_z[1], along_z[-1])
    near_y = [device(yl=flip(yl, k)) for k in (1, 2, 3)]
    far_y = device(yh=1 - yh)
    row_places = [(flip(x, k) if k else x, c) for k, c in ((2, 1 - core), (2, core), (1, 1 - core), (3, 1 - core), (1, core), (3, core), (0, 1 - core))]
    near_row = [device(x=there, core=c) for there, c in row_places]
    partners = [*along_z.values(), *near_y, far_y, *near_row]

    copies = Copies(extent, send_sem, recv_sem)
    copy = copies.start

    def arrived(*groups):
        copies.arrived(near_z[0], *groups)

    def at_z(at):
        return at // 4, lax.rem(at // 2, 2), lax.rem(at, 2)

    loads = [
        pltpu.make_async_copy(src, dst, local_sem.at[i])
        for i, (src, dst) in enumerate(
            [
                (fwd_hbm, xf.at[(yl, *at_z(z))]), (pre_hbm, pre), (up_hbm, up), (w_hbm, w),
                (bwd_hbm, xb.at[(yl, *at_z(z))]), (bias_hbm, bias),
            ]
        )
    ]
    barrier = pltpu.get_barrier_semaphore()
    for d in partners:
        pl.semaphore_signal(barrier, inc=1, device_id=d, device_id_type=MESH)
    for c in loads:
        c.start()
    loads[1].wait()
    loads[2].wait()
    g[yh, x, core] = (up[...].astype(F32) * gelu_slope(pre[...].astype(F32))).astype(BF16)
    pl.semaphore_wait(barrier, len(partners))

    waited = {1, 2}

    def loaded(*which):
        for i in which:
            if i not in waited:
                waited.add(i)
                loads[i].wait()

    class Gather:
        def __init__(self, name, hbm, ref, z_first):
            self.name, self.hbm, self.ref, self.z_first = name, hbm, ref, z_first

        def line(self):
            if self.z_first:
                arrived((self.name, 1), (self.name, "rest"))
                loaded(4)
                block = src = self.ref.at[yl]
            else:
                block, src = self.ref.at[(yl, *at_z(z))], self.hbm
            for k in (1, 2, 3):
                copy(src, block, near_y[k - 1], (self.name, "line", 0 if self.z_first else min(k, 2)))

        def block(self, which, source):
            if which == 0:
                return self.ref.at[(yl, *at_z(source))]
            rows = pl.ds(mate, 1) if which == 1 else pl.ds(2 * opposite, 2)
            return self.ref.at[(rows, *at_z(source))]

        def step(self, s, which, way):
            if s == 0:
                if which:
                    arrived((self.name, "line", which))
                block = self.block(which, z)
                src = block if which else self.hbm
                for way in (0, 1):
                    copy(src, block, along_z[(2, -2)[way]], (self.name, 2, which, way))
                for way in (0, 1):
                    copy(src, block, along_z[(1, -1)[way]], (self.name, 1))
                return
            arrived((self.name, 2, which, way))
            sign = (1, -1)[way]
            source = lax.rem(z - 2 * sign + 8, 8)
            if which == 2 or which == way:
                half = self.ref.at[(2 * opposite + way, *at_z(source))] if which == 2 else self.block(which, source)
                copy(half, half, along_z[2 * sign], (self.name, "rest"))
            block = self.block(which, source)
            copy(block, block, along_z[sign], (self.name, "rest"))

        def near(self):
            arrived((self.name, 1), *((self.name, 2, which, way) for which in (0, 1, 2) for way in (0, 1)))

        def finish(self):
            arrived((self.name, "line", 0) if self.z_first else (self.name, "rest"))

    gathers = {"f": Gather("f", fwd_hbm, xf, False), "b": Gather("b", bwd_hbm, xb, True)}

    def far():
        copy(g.at[yh, x, core], g.at[yh, x, core], far_y, "far")

    def spread(half):
        if half == 1:
            arrived("far")
        at = (yh, 1 - yh)[half]
        for d in near_row:
            copy(g.at[at, x, core], g.at[at, x, core], d, ("spread", half))

    halves = (yh, 1 - yh)

    def back(part):
        arrived(("spread", part))
        loaded(3)
        j = halves[part]
        rows = g[j].reshape(256, 768)

        def body(n, carry):
            at = pl.ds(pl.multiple_of(n * TILE, TILE), TILE)
            q[pl.ds(2 * j, 2), :, :, at] = lax.dot_general(
                rows, w[at, :], (((1,), (1,)), ((), ())), preferred_element_type=F32
            ).reshape(2, 8, 16, TILE)
            return carry

        lax.fori_loop(0, 2, body, 0)

    def rs_send(name, part, way, value, away, group):
        slots = pl.ds(RS_SLOT[name] + 7 * (2 * part + way), value.shape[0])
        rs_out[slots] = value.astype(BF16)
        copy(rs_out.at[slots], rs_in.at[slots], along_z[away], group)

    def rs_got(name, part, way):
        return rs_in[pl.ds(RS_SLOT[name] + 7 * (2 * part + way), RS_SIZE[name])].astype(F32)

    def rs(s, part, way):
        j, sign = halves[part], (1, -1)[way]

        def sums_for(away):
            return q[pl.ds(2 * j, 2), lax.rem(z + sign * away + 8, 8)]

        if s == 0:
            rs_send("three", part, way, sums_for(3), sign, ("mid", part, way))
            rs_send("four", part, way, q[pl.ds(2 * j + way, 1), lax.rem(z + 4, 8)], 2 * sign, ("mid", part, way))
            rs_send("one", part, way, sums_for(1), sign, ("end", part))
        else:
            arrived(("mid", part, way))
            value = sums_for(2) + rs_got("three", part, way)
            more = rs_got("four", part, way)
            parts = [value[:1] + more, value[1:]] if way == 0 else [value[:1], value[1:] + more]
            rs_send("two", part, way, jnp.concatenate(parts, axis=0), 2 * sign, ("end", part))

    def rsend(part):
        arrived(("end", part))
        value = q[pl.ds(2 * halves[part], 2), z]
        for way in (0, 1):
            value = value + rs_got("one", part, way) + rs_got("two", part, way)
        q[pl.ds(2 * halves[part], 2), z] = value

    def rsline():
        for k in (1, 2, 3):
            line_out[k - 1] = q[flip(yl, k), z].astype(BF16)
            copy(line_out.at[k - 1], line_in.at[k - 1], near_y[k - 1], "line")

    def igrad():
        arrived("line")
        igrad_ref[...] = (
            q[yl, z] + line_in[0].astype(F32) + line_in[1].astype(F32) + line_in[2].astype(F32)
        ).astype(BF16)

    odd = lax.rem(z, 2)
    near_pairs = (z // 2, lax.rem(z // 2 + 2 * odd + 3, 4))
    far_pairs = (lax.rem(z // 2 + 2, 4), lax.rem(z // 2 + 5 - 2 * odd, 4))

    def block_of(part, there, c):
        return 2 * (1 - yh, yh)[part] + there // 2, 2 * lax.rem(there, 2) + c

    def fwd(phase):
        loaded(0, 3)
        if phase == 0:
            gathers["f"].near()
        else:
            gathers["f"].finish()
        pairs = (near_pairs, far_pairs)[phase]
        rows = jnp.concatenate([xf[:, pair // 2, lax.rem(pair, 2)].reshape(128, 768) for pair in pairs], axis=0)

        def body(n, carry):
            at = pl.ds(pl.multiple_of(n * TILE, TILE), TILE)
            value = jnp.dot(rows, w[:, at], preferred_element_type=F32).reshape(2, 4, 32, TILE)
            for i, pair in enumerate(pairs):
                p[:, pair, :, at] = value[i]
                x_out[:, pair, :, at] = value[i].astype(BF16)
            return carry

        lax.fori_loop(0, 2, body, 0)
        for part in (0, 1):
            for i, ((there, c), d) in enumerate(zip(row_places, near_row)):
                at = block_of(part, there, c)

                @pl.when((at[1] == pairs[0]) | (at[1] == pairs[1]))
                def _():
                    copy(x_out.at[at], x_in.at[part, i], d, ("x", part), again=phase == 1)

    def fsum(part):
        arrived(("x", part))
        value = p[block_of(part, x, core)]
        for i in range(7):
            value = value + x_in[part, i].astype(F32)
        if part == 0:
            y_out[...] = value.astype(BF16)
            copy(y_out, y_in, far_y, "y")
        else:
            sums[...] = value

    def hid():
        loaded(5)
        arrived("y")
        hidden_ref[...] = gelu_tanh(sums[...] + y_in[...].astype(F32) + bias[...]).astype(BF16)

    def bg():
        bgrad_ref[...] = jnp.sum(g[...].reshape(512, 768).astype(F32), axis=0)

    def wg():
        gathers["b"].finish()
        loaded(4)

        def body(n, carry):
            at = pl.ds(pl.multiple_of(n * TILE, TILE), TILE)
            wgrad_ref[at, :] = lax.dot_general(
                xb[:, :, :, :, :, at].reshape(512, TILE), g[...].reshape(512, 768), (((0,), (0,)), ((), ())),
                preferred_element_type=F32,
            )
            return carry

        lax.fori_loop(0, 2, body, 0)

    single = dict(
        far=far, spread=spread, back=back, rs=rs, rsend=rsend, rsline=rsline, igrad=igrad,
        fwd=fwd, fsum=fsum, hid=hid, bg=bg, wg=wg,
    )
    for what, *at in ORDER:
        if what in gathers:
            if at == ["line"]:
                gathers[what].line()
            else:
                gathers[what].step(*at)
        else:
            single[what](*at)
    copies.finish(near_z[0])


def finish(*refs):
    sem = refs[-1]
    moves = [pltpu.make_async_copy(refs[i], refs[4 + i], sem.at[i]) for i in range(4)]
    for c in moves:
        c.start()
    for c in moves:
        c.wait()


def local(tokens_fwd, tokens_bwd, weight, bias, preact, upstream):
    hbm = pl.BlockSpec(memory_space=pltpu.HBM)
    vmem = pl.BlockSpec(memory_space=pltpu.VMEM)
    shapes = (
        jax.ShapeDtypeStruct((32, 768), BF16),
        jax.ShapeDtypeStruct((16, 768), BF16),
        jax.ShapeDtypeStruct((768, 768), F32),
        jax.ShapeDtypeStruct((768,), F32),
    )
    tokens_fwd, tokens_bwd, weight, bias, preact, upstream = [
        pltpu.with_memory_space_constraint(a, pltpu.HBM)
        for a in (tokens_fwd, tokens_bwd, weight, bias, preact, upstream)
    ]
    results = pl.pallas_call(
        kernel,
        out_shape=shapes,
        in_specs=[hbm] * 6,
        out_specs=[vmem] * 4,
        scratch_shapes=[
            pltpu.VMEM((4, 2, 2, 2, 16, 768), BF16),
            pltpu.VMEM((4, 2, 2, 2, 16, 768), BF16),
            pltpu.VMEM((2, 4, 2, 32, 768), BF16),
            pltpu.VMEM((4, 8, 16, 768), F32),
            pltpu.VMEM((768, 768), BF16),
            pltpu.VMEM((768,), F32),
            pltpu.VMEM((32, 768), BF16),
            pltpu.VMEM((32, 768), BF16),
            pltpu.VMEM((4, 4, 32, 768), F32),
            pltpu.VMEM((4, 4, 32, 768), BF16),
            pltpu.VMEM((2, 7, 32, 768), BF16),
            pltpu.VMEM((32, 768), BF16),
            pltpu.VMEM((32, 768), BF16),
            pltpu.VMEM((28, 16, 768), BF16),
            pltpu.VMEM((28, 16, 768), BF16),
            pltpu.VMEM((3, 16, 768), BF16),
            pltpu.VMEM((3, 16, 768), BF16),
            pltpu.VMEM((32, 768), F32),
            pltpu.VMEM((SENT_ROWS, 768), BF16),
            pltpu.SemaphoreType.DMA((N_LOCAL,)),
            pltpu.SemaphoreType.DMA,
            pltpu.SemaphoreType.DMA((N_GROUPS,)),
        ],
        compiler_params=pltpu.CompilerParams(
            collective_id=0, has_side_effects=True, vmem_limit_bytes=48 * 2**20
        ),
        cost_estimate=pl.CostEstimate(flops=3 * 2 * 512 * 768 * 768, bytes_accessed=8 * 2**20, transcendentals=50000),
        name="feed_forward",
    )(tokens_fwd, tokens_bwd, weight, bias, preact, upstream)
    return pl.pallas_call(
        finish,
        out_shape=tuple(jax.ShapeDtypeStruct(r.shape, r.dtype) for r in results),
        in_specs=[pl.BlockSpec(memory_space=pltpu.VMEM)] * 4,
        out_specs=[pl.BlockSpec(memory_space=pl.ANY)] * 4,
        scratch_shapes=[pltpu.SemaphoreType.DMA((4,))],
        compiler_params=pltpu.CompilerParams(vmem_limit_bytes=1 << 20),
        name="write_out",
    )(*results)

def solution(mesh):
    return jax.shard_map(
        local,
        mesh=mesh,
        in_specs=(
            P("col", "row"),
            P("col", "row"),
            P("row", "col"),
            P("col"),
            P("row", "col"),
            P("row", "col"),
        ),
        out_specs=(P("row", "col"), P("col", "row"), P("row", "col"), P("col")),
        check_vma=False,
    )
```

```python
import math

import jax
import jax.numpy as jnp
from jax import lax
from jax.experimental import pallas as pl
from jax.experimental.pallas import tpu as pltpu
from jax.sharding import PartitionSpec as P

gelu_scale = math.sqrt(2.0 / math.pi)
cubic_term = 0.044715
F32, BF16 = jnp.float32, jnp.bfloat16
MESH = pl.DeviceIdType.MESH
TILE = 384


def gelu_tanh(values):
    inner_arg = gelu_scale * (values + cubic_term * values * values * values)
    return 0.5 * values * (1.0 + jnp.tanh(inner_arg))


def gelu_slope(values):
    tangent = jnp.tanh(gelu_scale * (values + cubic_term * values * values * values))
    return 0.5 * (1.0 + tangent) + 0.5 * values * (1.0 - tangent * tangent) * gelu_scale * (
        1.0 + 3.0 * cubic_term * values * values
    )


def flip(i, k):
    if k == 1:
        return i + 1 - 2 * lax.rem(i, 2)
    if k == 2:
        return lax.rem(i + 2, 4)
    return 3 - i


class Copies:
    def __init__(self, extent, send, recv):
        self.extent, self.send, self.recv = extent, send, recv
        self.groups, self.waited, self.sent = {}, set(), 0

    def start(self, src, dst, target, group, again=False):
        rows = 0 if again else math.prod(dst.shape) // 768
        number, before = self.groups.get(group, (len(self.groups), 0))
        self.groups[group] = (number, before + rows)
        self.sent += rows
        pltpu.make_async_remote_copy(
            src_ref=src, dst_ref=dst, send_sem=self.send, recv_sem=self.recv.at[number],
            device_id=target, device_id_type=MESH,
        ).start()

    def whole(self, rows, number, target):
        extent = self.extent.at[pl.ds(0, rows)]
        return pltpu.make_async_remote_copy(
            src_ref=extent, dst_ref=extent, send_sem=self.send, recv_sem=self.recv.at[number],
            device_id=target, device_id_type=MESH,
        )

    def arrived(self, target, *groups):
        for group in groups:
            if group not in self.waited:
                self.waited.add(group)
                number, rows = self.groups[group]
                self.whole(rows, number, target).wait_recv()

    def finish(self, target):
        self.whole(self.sent, 0, target).wait_send()


ORDER = (
    ("f", "line"), ("f", 0, 0, 0), ("grad",), ("far",), ("spread", 0), ("b", 0, 0, 0), ("f", 0, 1, 0),
    ("b", 1, 0, 0), ("b", 1, 0, 1), ("f", 0, 2, 0), ("spread", 1), ("back", 0), ("rs", 0, 0, 1), ("b", "line"),
    ("f", 1, 0, 0), ("f", 1, 2, 1), ("f", 1, 0, 1), ("f", 1, 1, 1), ("f", 1, 1, 0), ("f", 1, 2, 0), ("rs", 0, 0, 0),
    ("fwd", 0), ("back", 1), ("rs", 0, 1, 0), ("rs", 0, 1, 1), ("fwd", 1), ("rs", 1, 0, 1), ("rs", 1, 0, 0),
    ("rs", 1, 1, 0), ("rs", 1, 1, 1), ("fsum", 0), ("bg",), ("rsend", 0), ("rsend", 1), ("rsline",), ("wg",),
    ("fsum", 1), ("hid",), ("igrad",),
)


RS_SLOT = {"three": 0, "four": 2, "one": 3, "two": 5}
RS_SIZE = {"three": 2, "four": 1, "one": 2, "two": 2}
N_LOCAL = 6
N_GROUPS = 28
SENT_ROWS = 2448


def kernel(
    fwd_hbm, bwd_hbm, w_hbm, bias_hbm, pre_hbm, up_hbm,
    hidden_ref, igrad_ref, wgrad_ref, bgrad_ref,
    xf, xb, g, q, w, bias, pre, up,
    p, x_out, x_in, y_out, y_in,
    rs_out, rs_in, line_out, line_in, sums,
    extent, local_sem, send_sem, recv_sem,
):
    row, col = lax.axis_index("row"), lax.axis_index("col")
    yh, x, core = row // 8, lax.rem(row // 2, 4), lax.rem(row, 2)
    yl, z = col // 8, lax.rem(col, 8)
    mate, opposite = flip(yl, 1), 1 - yl // 2

    def device(yh=yh, x=x, core=core, yl=yl, z=z):
        return (yh * 8 + x * 2 + core, yl * 8 + z)

    along_z = {away: device(z=lax.rem(z + away + 8, 8)) for away in (1, -1, 2, -2)}
    near_z = (along_z[1], along_z[-1])
    near_y = [device(yl=flip(yl, k)) for k in (1, 2, 3)]
    far_y = device(yh=1 - yh)
    row_places = [(flip(x, k) if k else x, c) for k, c in ((2, 1 - core), (2, core), (1, 1 - core), (3, 1 - core), (1, core), (3, core), (0, 1 - core))]
    near_row = [device(x=there, core=c) for there, c in row_places]
    partners = [*along_z.values(), *near_y, far_y, *near_row]

    copies = Copies(extent, send_sem, recv_sem)
    copy = copies.start

    def arrived(*groups):
        copies.arrived(near_z[0], *groups)

    def at_z(at):
        return at // 4, lax.rem(at // 2, 2), lax.rem(at, 2)

    loads = [
        pltpu.make_async_copy(src, dst, local_sem.at[i])
        for i, (src, dst) in enumerate(
            [
                (fwd_hbm, xf.at[(yl, *at_z(z))]), (pre_hbm, pre), (up_hbm, up), (w_hbm, w),
                (bwd_hbm, xb.at[(yl, *at_z(z))]), (bias_hbm, bias),
            ]
        )
    ]
    barrier = pltpu.get_barrier_semaphore()
    for d in partners:
        pl.semaphore_signal(barrier, inc=1, device_id=d, device_id_type=MESH)
    for c in loads:
        c.start()
    pl.semaphore_wait(barrier, len(partners))

    waited = set()

    def loaded(*which):
        for i in which:
            if i not in waited:
                waited.add(i)
                loads[i].wait()

    class Gather:
        def __init__(self, name, hbm, ref, z_first):
            self.name, self.hbm, self.ref, self.z_first = name, hbm, ref, z_first

        def line(self):
            if self.z_first:
                arrived((self.name, 1), (self.name, "rest"))
                loaded(4)
                block = src = self.ref.at[yl]
            else:
                block, src = self.ref.at[(yl, *at_z(z))], self.hbm
            for k in (1, 2, 3):
                copy(src, block, near_y[k - 1], (self.name, "line", 0 if self.z_first else min(k, 2)))

        def block(self, which, source):
            if which == 0:
                return self.ref.at[(yl, *at_z(source))]
            rows = pl.ds(mate, 1) if which == 1 else pl.ds(2 * opposite, 2)
            return self.ref.at[(rows, *at_z(source))]

        def step(self, s, which, way):
            if s == 0:
                if which:
                    arrived((self.name, "line", which))
                block = self.block(which, z)
                src = block if which else self.hbm
                for way in (0, 1):
                    copy(src, block, along_z[(2, -2)[way]], (self.name, 2, which, way))
                for way in (0, 1):
                    copy(src, block, along_z[(1, -1)[way]], (self.name, 1))
                return
            arrived((self.name, 2, which, way))
            sign = (1, -1)[way]
            source = lax.rem(z - 2 * sign + 8, 8)
            if which == 2 or which == way:
                half = self.ref.at[(2 * opposite + way, *at_z(source))] if which == 2 else self.block(which, source)
                copy(half, half, along_z[2 * sign], (self.name, "rest"))
            block = self.block(which, source)
            copy(block, block, along_z[sign], (self.name, "rest"))

        def near(self):
            arrived((self.name, 1), *((self.name, 2, which, way) for which in (0, 1, 2) for way in (0, 1)))

        def finish(self):
            arrived((self.name, "line", 0) if self.z_first else (self.name, "rest"))

    gathers = {"f": Gather("f", fwd_hbm, xf, False), "b": Gather("b", bwd_hbm, xb, True)}

    def grad():
        loaded(1, 2)
        g[yh, x, core] = (up[...].astype(F32) * gelu_slope(pre[...].astype(F32))).astype(BF16)

    def far():
        copy(g.at[yh, x, core], g.at[yh, x, core], far_y, "far")

    def spread(half):
        if half == 1:
            arrived("far")
        at = (yh, 1 - yh)[half]
        for d in near_row:
            copy(g.at[at, x, core], g.at[at, x, core], d, ("spread", half))

    halves = (yh, 1 - yh)

    def back(part):
        arrived(("spread", part))
        loaded(3)
        j = halves[part]
        rows = g[j].reshape(256, 768)

        def body(n, carry):
            at = pl.ds(pl.multiple_of(n * TILE, TILE), TILE)
            q[pl.ds(2 * j, 2), :, :, at] = lax.dot_general(
                rows, w[at, :], (((1,), (1,)), ((), ())), preferred_element_type=F32
            ).reshape(2, 8, 16, TILE)
            return carry

        lax.fori_loop(0, 2, body, 0)

    def rs_send(name, part, way, value, away, group):
        slots = pl.ds(RS_SLOT[name] + 7 * (2 * part + way), value.shape[0])
        rs_out[slots] = value.astype(BF16)
        copy(rs_out.at[slots], rs_in.at[slots], along_z[away], group)

    def rs_got(name, part, way):
        return rs_in[pl.ds(RS_SLOT[name] + 7 * (2 * part + way), RS_SIZE[name])].astype(F32)

    def rs(s, part, way):
        j, sign = halves[part], (1, -1)[way]

        def sums_for(away):
            return q[pl.ds(2 * j, 2), lax.rem(z + sign * away + 8, 8)]

        if s == 0:
            rs_send("three", part, way, sums_for(3), sign, ("mid", part, way))
            rs_send("four", part, way, q[pl.ds(2 * j + way, 1), lax.rem(z + 4, 8)], 2 * sign, ("mid", part, way))
            rs_send("one", part, way, sums_for(1), sign, ("end", part))
        else:
            arrived(("mid", part, way))
            value = sums_for(2) + rs_got("three", part, way)
            more = rs_got("four", part, way)
            parts = [value[:1] + more, value[1:]] if way == 0 else [value[:1], value[1:] + more]
            rs_send("two", part, way, jnp.concatenate(parts, axis=0), 2 * sign, ("end", part))

    def rsend(part):
        arrived(("end", part))
        value = q[pl.ds(2 * halves[part], 2), z]
        for way in (0, 1):
            value = value + rs_got("one", part, way) + rs_got("two", part, way)
        q[pl.ds(2 * halves[part], 2), z] = value

    def rsline():
        for k in (1, 2, 3):
            line_out[k - 1] = q[flip(yl, k), z].astype(BF16)
            copy(line_out.at[k - 1], line_in.at[k - 1], near_y[k - 1], "line")

    def igrad():
        arrived("line")
        igrad_ref[...] = (
            q[yl, z] + line_in[0].astype(F32) + line_in[1].astype(F32) + line_in[2].astype(F32)
        ).astype(BF16)

    odd = lax.rem(z, 2)
    near_pairs = (z // 2, lax.rem(z // 2 + 2 * odd + 3, 4))
    far_pairs = (lax.rem(z // 2 + 2, 4), lax.rem(z // 2 + 5 - 2 * odd, 4))

    def block_of(part, there, c):
        return 2 * (1 - yh, yh)[part] + there // 2, 2 * lax.rem(there, 2) + c

    def fwd(phase):
        loaded(0, 3)
        if phase == 0:
            gathers["f"].near()
        else:
            gathers["f"].finish()
        pairs = (near_pairs, far_pairs)[phase]
        rows = jnp.concatenate([xf[:, pair // 2, lax.rem(pair, 2)].reshape(128, 768) for pair in pairs], axis=0)

        def body(n, carry):
            at = pl.ds(pl.multiple_of(n * TILE, TILE), TILE)
            value = jnp.dot(rows, w[:, at], preferred_element_type=F32).reshape(2, 4, 32, TILE)
            for i, pair in enumerate(pairs):
                p[:, pair, :, at] = value[i]
                x_out[:, pair, :, at] = value[i].astype(BF16)
            return carry

        lax.fori_loop(0, 2, body, 0)
        for part in (0, 1):
            for i, ((there, c), d) in enumerate(zip(row_places, near_row)):
                at = block_of(part, there, c)

                @pl.when((at[1] == pairs[0]) | (at[1] == pairs[1]))
                def _():
                    copy(x_out.at[at], x_in.at[part, i], d, ("x", part), again=phase == 1)

    def fsum(part):
        arrived(("x", part))
        value = p[block_of(part, x, core)]
        for i in range(7):
            value = value + x_in[part, i].astype(F32)
        if part == 0:
            y_out[...] = value.astype(BF16)
            copy(y_out, y_in, far_y, "y")
        else:
            sums[...] = value

    def hid():
        loaded(5)
        arrived("y")
        hidden_ref[...] = gelu_tanh(sums[...] + y_in[...].astype(F32) + bias[...]).astype(BF16)

    def bg():
        bgrad_ref[...] = jnp.sum(g[...].reshape(512, 768).astype(F32), axis=0)

    def wg():
        gathers["b"].finish()
        loaded(4)

        def body(n, carry):
            at = pl.ds(pl.multiple_of(n * TILE, TILE), TILE)
            wgrad_ref[at, :] = lax.dot_general(
                xb[:, :, :, :, :, at].reshape(512, TILE), g[...].reshape(512, 768), (((0,), (0,)), ((), ())),
                preferred_element_type=F32,
            )
            return carry

        lax.fori_loop(0, 2, body, 0)

    single = dict(
        grad=grad, far=far, spread=spread, back=back, rs=rs, rsend=rsend, rsline=rsline, igrad=igrad,
        fwd=fwd, fsum=fsum, hid=hid, bg=bg, wg=wg,
    )
    for what, *at in ORDER:
        if what in gathers:
            if at == ["line"]:
                gathers[what].line()
            else:
                gathers[what].step(*at)
        else:
            single[what](*at)
    copies.finish(near_z[0])


def finish(*refs):
    sem = refs[-1]
    moves = [pltpu.make_async_copy(refs[i], refs[4 + i], sem.at[i]) for i in range(4)]
    for c in moves:
        c.start()
    for c in moves:
        c.wait()


def local(tokens_fwd, tokens_bwd, weight, bias, preact, upstream):
    hbm = pl.BlockSpec(memory_space=pltpu.HBM)
    vmem = pl.BlockSpec(memory_space=pltpu.VMEM)
    shapes = (
        jax.ShapeDtypeStruct((32, 768), BF16),
        jax.ShapeDtypeStruct((16, 768), BF16),
        jax.ShapeDtypeStruct((768, 768), F32),
        jax.ShapeDtypeStruct((768,), F32),
    )
    tokens_fwd, tokens_bwd, weight, bias, preact, upstream = [
        pltpu.with_memory_space_constraint(a, pltpu.HBM)
        for a in (tokens_fwd, tokens_bwd, weight, bias, preact, upstream)
    ]
    results = pl.pallas_call(
        kernel,
        out_shape=shapes,
        in_specs=[hbm] * 6,
        out_specs=[vmem] * 4,
        scratch_shapes=[
            pltpu.VMEM((4, 2, 2, 2, 16, 768), BF16),
            pltpu.VMEM((4, 2, 2, 2, 16, 768), BF16),
            pltpu.VMEM((2, 4, 2, 32, 768), BF16),
            pltpu.VMEM((4, 8, 16, 768), F32),
            pltpu.VMEM((768, 768), BF16),
            pltpu.VMEM((768,), F32),
            pltpu.VMEM((32, 768), BF16),
            pltpu.VMEM((32, 768), BF16),
            pltpu.VMEM((4, 4, 32, 768), F32),
            pltpu.VMEM((4, 4, 32, 768), BF16),
            pltpu.VMEM((2, 7, 32, 768), BF16),
            pltpu.VMEM((32, 768), BF16),
            pltpu.VMEM((32, 768), BF16),
            pltpu.VMEM((28, 16, 768), BF16),
            pltpu.VMEM((28, 16, 768), BF16),
            pltpu.VMEM((3, 16, 768), BF16),
            pltpu.VMEM((3, 16, 768), BF16),
            pltpu.VMEM((32, 768), F32),
            pltpu.VMEM((SENT_ROWS, 768), BF16),
            pltpu.SemaphoreType.DMA((N_LOCAL,)),
            pltpu.SemaphoreType.DMA,
            pltpu.SemaphoreType.DMA((N_GROUPS,)),
        ],
        compiler_params=pltpu.CompilerParams(
            collective_id=0, has_side_effects=True, vmem_limit_bytes=48 * 2**20
        ),
        cost_estimate=pl.CostEstimate(flops=3 * 2 * 512 * 768 * 768, bytes_accessed=8 * 2**20, transcendentals=50000),
        name="feed_forward",
    )(tokens_fwd, tokens_bwd, weight, bias, preact, upstream)
    return pl.pallas_call(
        finish,
        out_shape=tuple(jax.ShapeDtypeStruct(r.shape, r.dtype) for r in results),
        in_specs=[pl.BlockSpec(memory_space=pltpu.VMEM)] * 4,
        out_specs=[pl.BlockSpec(memory_space=pl.ANY)] * 4,
        scratch_shapes=[pltpu.SemaphoreType.DMA((4,))],
        compiler_params=pltpu.CompilerParams(vmem_limit_bytes=1 << 20),
        name="write_out",
    )(*results)

def solution(mesh):
    return jax.shard_map(
        local,
        mesh=mesh,
        in_specs=(
            P("col", "row"),
            P("col", "row"),
            P("row", "col"),
            P("col"),
            P("row", "col"),
            P("row", "col"),
        ),
        out_specs=(P("row", "col"), P("col", "row"), P("row", "col"), P("col")),
        check_vma=False,
    )
```
